128 devices in a mesh: ctx: 8 (over y_lo, x), resp: 16 (over z, y_hi, core).
Axes of the slice: x: 4, y: 4 (y_hi: 2, y_lo: 2; y = y_hi * 2 + y_lo), z: 4, core: 2. Of those that a mesh axis runs over, the one named last changes fastest.
Arguments:
- query: bfloat16 [16, 1024, 4096], P('resp', 'ctx'), may hold values from -12 to 12
- prompt_keys: bfloat16 [1024, 512], P('ctx'), may hold values from -12 to 12
- prompt_value_rows: bfloat16 [1024, 512], P('ctx'), may hold values from -6 to 6
- response_keys: bfloat16 [16, 1024, 512], P('resp', 'ctx'), may hold values from -6 to 6
- response_values: bfloat16 [16, 1024, 512], P('resp', 'ctx'), may hold values from -6 to 6
- d_out: bfloat16 [16, 1024, 4096], P('resp', 'ctx'), may hold values from -24 to 24
- lengths: int32 [16], P('resp'), may hold values from 256 to 1024, as said below
Outputs:
- d_query: bfloat16 [16, 1024, 4096], P('resp', 'ctx')
- d_resp_keys: bfloat16 [16, 1024, 512], P('resp', 'ctx')
- d_resp_values: bfloat16 [16, 1024, 512], P('resp', 'ctx')
- d_prompt_keys: bfloat16 [1024, 512], P(('ctx', 'resp'))
- d_prompt_values: bfloat16 [1024, 512], P(('ctx', 'resp'))
The draws below stay inside these ranges and needn't reach their ends.
Inputs may be any that keep to these rules, and one draw needn't show every extreme that they name: `lengths`: every draw has some response of 1024 live tokens.
All inputs are finite; a program needn't handle non-finite values.
Results may differ from the reference program's by a relative error of at most 0.017.
Values may be sent and summed in bfloat16 or wider, within the bound.
A program may use at most 128 MiB of HBM per device.

```python
import jax
import jax.numpy as jnp
from jax import lax

QUERY_HEADS = 32
KEY_VALUE_HEADS = 4
HEAD_SIZE = 128
RESPONSE_PER_CTX = 128
PROMPT_LENGTH = 1024
RESPONSE_SLOTS = 1024
RESPONSE_COUNT = 16
N_CTX = 8


def draw_prompt_keys(key, part):
    key = jax.random.fold_in(key, 1)
    sampled_values = jnp.clip(jax.random.normal(key, (PROMPT_LENGTH, KEY_VALUE_HEADS * HEAD_SIZE), jnp.float32), -6.0, 6.0)
    return sampled_values.astype(jnp.bfloat16)


def draw_query(key, part):
    key = jax.random.fold_in(key, 2)
    sampled_values = jnp.clip(1.5 * jax.random.normal(key, (RESPONSE_COUNT, RESPONSE_SLOTS, QUERY_HEADS * HEAD_SIZE), jnp.float32), -6.0, 6.0)
    return sampled_values.astype(jnp.bfloat16)


def draw_lengths(key, part):
    key = jax.random.fold_in(key, 3)
    sampled_values = jax.random.randint(key, (RESPONSE_COUNT,), RESPONSE_SLOTS // 4, RESPONSE_SLOTS + 1, dtype=jnp.int32)
    chosen = jax.random.randint(jax.random.fold_in(key, 4), (), 0, RESPONSE_COUNT, dtype=jnp.int32)
    return sampled_values.at[chosen].set(RESPONSE_SLOTS)


def shard_levels(own_key, shape, split, smallest, high):
    factor_of, own = 1.0, jax.random.fold_in(own_key, 6)
    for axis_at, shards_of in split:
        draws = jnp.exp(jax.random.uniform(jax.random.fold_in(own, axis_at), (shards_of,), jnp.float32, smallest / len(split), high / len(split)))
        factor_of = factor_of * jnp.repeat(draws, shape[axis_at] // shards_of).reshape([-1 if axis == axis_at else 1 for axis in range(len(shape))])
    return factor_of


def gaussian(key, extent, width, reach, split=(), kind=jnp.bfloat16):
    loudness = shard_levels(key, extent, split, -0.22, 0.18) if split else 1.0
    drawn = jax.random.normal(key, extent, jnp.float32) * width * loudness
    return jnp.minimum(jnp.maximum(drawn, -reach), reach).astype(kind)


def setup_inputs(seed: int = 0) -> dict:
    key_of = jax.random.split(jax.random.key(seed), 8)
    return {
        "query": draw_query(jax.random.fold_in(key_of[7], 71), 0),
        "prompt_keys": draw_prompt_keys(jax.random.fold_in(key_of[7], 71), 0),
        "prompt_value_rows": gaussian(key_of[2], (PROMPT_LENGTH, KEY_VALUE_HEADS * HEAD_SIZE), 1.0, 6.0, ((0, 8),)),
        "response_keys": gaussian(key_of[3], (RESPONSE_COUNT, RESPONSE_SLOTS, KEY_VALUE_HEADS * HEAD_SIZE), 1.0, 6.0, ((0, 16), (1, 8))),
        "response_values": gaussian(key_of[4], (RESPONSE_COUNT, RESPONSE_SLOTS, KEY_VALUE_HEADS * HEAD_SIZE), 1.0, 6.0, ((0, 16), (1, 8))),
        "d_out": gaussian(key_of[5], (RESPONSE_COUNT, RESPONSE_SLOTS, QUERY_HEADS * HEAD_SIZE), 4.0, 24.0, ((0, 16), (1, 8))),
        "lengths": draw_lengths(jax.random.fold_in(key_of[7], 71), 0),
    }


def rounded(values):
    return lax.optimization_barrier(values.astype(jnp.bfloat16)).astype(jnp.float32)


def block_terms(query_head_count, g_heads, key_matrix, value_matrix, allowed):
    highest = lax.Precision.HIGHEST
    scale_factor = HEAD_SIZE ** -0.5
    scores = jnp.einsum('rhgd,nhd->hgrn', query_head_count, key_matrix, precision=highest) * scale_factor
    scores = jnp.where(allowed, scores, -jnp.inf)
    row_max = jnp.max(scores, axis=-1, keepdims=True)
    log_total = row_max + jnp.log(jnp.sum(jnp.exp(scores - row_max), axis=-1, keepdims=True))
    probs = jnp.exp(scores - log_total)
    probs_low = rounded(probs)
    attended = jnp.einsum('hgrn,nhd->hgrd', probs_low, value_matrix, precision=highest)
    delta_row = jnp.einsum('rhgd,hgrd->hgr', g_heads, attended, precision=highest)
    d_probs = jnp.einsum('rhgd,nhd->hgrn', g_heads, value_matrix, precision=highest)
    d_scores = rounded(probs * (d_probs - delta_row[..., None]))
    d_queries = jnp.einsum('hgrn,nhd->rhgd', d_scores, key_matrix, precision=highest) * scale_factor
    d_keys = jnp.einsum('hgrn,rhgd->nhd', d_scores, query_head_count, precision=highest) * scale_factor
    d_values = jnp.einsum('hgrn,rhgd->nhd', probs_low, g_heads, precision=highest)
    return d_queries, d_keys, d_values


def reference(query, prompt_keys, prompt_value_rows, response_keys, response_values, d_out, lengths):
    query_group_size = QUERY_HEADS // KEY_VALUE_HEADS
    feature_width = KEY_VALUE_HEADS * HEAD_SIZE
    prompt_key_block = prompt_keys.astype(jnp.float32)
    prompt_value_block = prompt_value_rows.astype(jnp.float32)

    def one_response(carried, inputs):
        prompt_dk, prompt_dv = carried
        query_matrix, response_key_block, response_value_block, grad_rows, live_count = inputs
        key_matrix = jnp.concatenate([prompt_key_block, response_key_block.astype(jnp.float32)], axis=0).reshape(PROMPT_LENGTH + RESPONSE_SLOTS, KEY_VALUE_HEADS, HEAD_SIZE)
        value_matrix = jnp.concatenate([prompt_value_block, response_value_block.astype(jnp.float32)], axis=0).reshape(PROMPT_LENGTH + RESPONSE_SLOTS, KEY_VALUE_HEADS, HEAD_SIZE)
        live_rows = jnp.arange(RESPONSE_SLOTS) < live_count
        masked_gradient = jnp.where(live_rows[:, None], grad_rows.astype(jnp.float32), jnp.float32(0.0))
        query_blocks = query_matrix.astype(jnp.float32).reshape(N_CTX, RESPONSE_PER_CTX, KEY_VALUE_HEADS, query_group_size, HEAD_SIZE)
        gradient_blocks = masked_gradient.reshape(N_CTX, RESPONSE_PER_CTX, KEY_VALUE_HEADS, query_group_size, HEAD_SIZE)
        columns = jnp.arange(PROMPT_LENGTH + RESPONSE_SLOTS)

        def one_block(inner, block_inputs):
            acc_k, acc_v, resp_dk, resp_dv = inner
            q_block, g_block, block_index = block_inputs
            rows_at = block_index * RESPONSE_PER_CTX + jnp.arange(RESPONSE_PER_CTX)
            allowed = (columns[None, :] < PROMPT_LENGTH) | (columns[None, :] - PROMPT_LENGTH <= rows_at[:, None])
            d_queries, d_keys, d_values = block_terms(q_block, g_block, key_matrix, value_matrix, allowed)
            new_inner = (acc_k + d_keys[:PROMPT_LENGTH], acc_v + d_values[:PROMPT_LENGTH],
                         resp_dk + rounded(d_keys[PROMPT_LENGTH:]), resp_dv + rounded(d_values[PROMPT_LENGTH:]))
            return new_inner, d_queries

        inner_begin = (jnp.zeros((PROMPT_LENGTH, KEY_VALUE_HEADS, HEAD_SIZE), jnp.float32), jnp.zeros((PROMPT_LENGTH, KEY_VALUE_HEADS, HEAD_SIZE), jnp.float32),
                       jnp.zeros((RESPONSE_SLOTS, KEY_VALUE_HEADS, HEAD_SIZE), jnp.float32), jnp.zeros((RESPONSE_SLOTS, KEY_VALUE_HEADS, HEAD_SIZE), jnp.float32))
        inner, d_queries = lax.scan(one_block, inner_begin, (query_blocks, gradient_blocks, jnp.arange(N_CTX)))
        acc_k, acc_v, resp_dk, resp_dv = inner
        new_carried = (prompt_dk + acc_k.reshape(PROMPT_LENGTH, feature_width), prompt_dv + acc_v.reshape(PROMPT_LENGTH, feature_width))
        outputs = (d_queries.reshape(RESPONSE_SLOTS, QUERY_HEADS * HEAD_SIZE).astype(jnp.bfloat16),
                   resp_dk.reshape(RESPONSE_SLOTS, feature_width).astype(jnp.bfloat16),
                   resp_dv.reshape(RESPONSE_SLOTS, feature_width).astype(jnp.bfloat16))
        return new_carried, outputs

    start = (jnp.zeros((PROMPT_LENGTH, feature_width), jnp.float32), jnp.zeros((PROMPT_LENGTH, feature_width), jnp.float32))
    totals, outputs = lax.scan(one_response, start, (query, response_keys, response_values, d_out, lengths))
    d_query, d_resp_keys, d_resp_values = outputs
    return (d_query, d_resp_keys, d_resp_values,
            totals[0].astype(jnp.bfloat16), totals[1].astype(jnp.bfloat16))
```

```python
import functools

import jax
import jax.numpy as jnp
from jax import lax
from jax.experimental import pallas as pl
from jax.experimental.pallas import tpu as pltpu
from jax.sharding import PartitionSpec as P

F32, BF16 = jnp.float32, jnp.bfloat16
MESH = pl.DeviceIdType.MESH
SCALE = 128 ** -0.5
EXP2_SCALE = SCALE * 1.4426950408889634
BLOCK = 16


def dot(a, b):
    return lax.dot_general(a, b, (((1,), (0,)), ((), ())), preferred_element_type=F32)


def aligned(x, n):
    return x if isinstance(x, int) else pl.multiple_of(x, n)


def wait_bytes(ref, sem):
    pltpu.make_async_copy(ref, ref, sem).wait()


def kernel(
    q_hbm, pk_hbm, pv_hbm, rk_hbm, rv_hbm, g_hbm, len_ref,
    dq_hbm, drk_ref, drv_ref, dpk_ref, dpv_ref,
    q, gm, dq, pstage, kv, term, back, half_in, half_sum, z_in, plane_out, plane_in,
    pt0, pt1, ds0, ds1, s0, s1, dp0, dp1, kt0, kt1, vt0, vt1, qst, gst, bias,
    loc_sem, out_sem, p_send, p_recv, f_send, f_recv, r_send, r_recv, d_send, d_recv,
    h_send, h_recv, z_send, z_recv, x_send, x_recv,
):
    c, r = lax.axis_index("ctx"), lax.axis_index("resp")
    y_lo, x = c // 4, c % 4
    z, y_hi, core = r // 4, (r // 2) % 2, r % 2
    sibling = (c, z * 4 + y_hi * 2 + 1 - core)
    other = 1 - core
    PT, DS, KT, VT, S, DP = [pt0, pt1], [ds0, ds1], [kt0, kt1], [vt0, vt1], [s0, s1], [dp0, dp1]

    loads = []
    for g in range(4):
        cols = pl.ds(g * 128, 128)
        loads.append(pltpu.make_async_copy(rk_hbm.at[:, cols], kv.at[g, 0, 8], loc_sem.at[len(loads)]))
        loads.append(pltpu.make_async_copy(rv_hbm.at[:, cols], kv.at[g, 1, 8], loc_sem.at[len(loads)]))
    loads.append(pltpu.make_async_copy(pk_hbm, pstage.at[0], loc_sem.at[8]))
    loads.append(pltpu.make_async_copy(pv_hbm, pstage.at[1], loc_sem.at[9]))
    q_load = pltpu.make_async_copy(q_hbm, q, loc_sem.at[10])
    g_load = pltpu.make_async_copy(g_hbm, gm, loc_sem.at[11])
    for copy in loads:
        copy.start()
    q_load.start()
    g_load.start()

    barrier = pltpu.get_barrier_semaphore()
    plane_id = c * 2 + y_hi

    def plane_device(step):
        to = (plane_id + step) % 16
        return to // 2, to % 2

    for step in range(1, 16):
        to_c, to_y = plane_device(step)
        pl.semaphore_signal(barrier, inc=1, device_id=(to_c, z * 4 + to_y * 2 + core), device_id_type=MESH)
    for step in range(1, 4):
        to_z = (z + step) % 4
        pl.semaphore_signal(barrier, inc=1, device_id=(c, to_z * 4 + y_hi * 2 + core), device_id_type=MESH)
    pl.semaphore_signal(barrier, inc=1, device_id=sibling, device_id_type=MESH)

    for copy in loads:
        copy.wait()
    for kind in range(2):
        rows = pstage[kind].astype(F32)
        order = [zz * 4 + yy * 2 + cc for cc in range(2) for zz in range(4) for yy in range(2)]
        mixed = jnp.concatenate([rows[8 * o : 8 * o + 8] for o in order], axis=0).astype(BF16)
        pstage[kind] = mixed
    for g in range(4):
        for kind in range(2):
            kv[g, kind, c, pl.ds(pl.multiple_of(core * 64, 64), 64), :] = pstage[
                kind, pl.ds(pl.multiple_of(core * 64, 64), 64), g * 128 : g * 128 + 128
            ]
    pl.semaphore_wait(barrier, 19)

    my_half = pl.ds(pl.multiple_of(core * 64, 64), 64)
    other_half = pl.ds(pl.multiple_of(other * 64, 64), 64)

    def prompt_copy(g, step):
        to_c = (c + step) % 8
        to_y = jnp.where(to_c // 4 == y_lo, y_hi, 1 - y_hi)
        return pltpu.make_async_remote_copy(
            src_ref=kv.at[g, :, c, my_half], dst_ref=kv.at[g, :, c, my_half],
            send_sem=p_send.at[g], recv_sem=p_recv.at[g],
            device_id=(to_c, z * 4 + to_y * 2 + core), device_id_type=MESH,
        )

    def resp_copy(g, step):
        return pltpu.make_async_remote_copy(
            src_ref=kv.at[g, :, 8], dst_ref=kv.at[g, :, 8 + step],
            send_sem=r_send.at[g, step], recv_sem=r_recv.at[g, step],
            device_id=(c + step, r), device_id_type=MESH,
        )

    def send_head(g):
        for step in range(1, 8):
            prompt_copy(g, step).start()
        for step in range(1, 8):
            @pl.when(c + step < 8)
            def _():
                resp_copy(g, step).start()

    def forward_copy(g):
        return pltpu.make_async_remote_copy(
            src_ref=kv.at[g, :, pl.ds(0, 8), my_half], dst_ref=kv.at[g, :, pl.ds(0, 8), my_half],
            send_sem=f_send.at[g], recv_sem=f_recv.at[g], device_id=sibling, device_id_type=MESH,
        )

    def forward_head(g):
        wait_bytes(kv.at[g, :, pl.ds(0, 7), my_half], p_recv.at[g])
        forward_copy(g).start()

    def await_head(g):
        for step in range(1, 8):
            @pl.when(step <= c)
            def _():
                wait_bytes(kv.at[g, :, 8 + step], r_recv.at[g, step])
        wait_bytes(kv.at[g, :, pl.ds(0, 8), other_half], f_recv.at[g])

    send_head(0)

    row = lax.broadcasted_iota(jnp.int32, (128, 1024), 0)
    key = lax.broadcasted_iota(jnp.int32, (128, 1024), 1)
    flag = ((key == row + 1) & (key < 128)) | ((row == 127) & (key >= (c + 1) * 128))
    flag = jnp.where(flag, 1.0, 0.0).astype(BF16)
    kt0[128:, 1024:] = flag
    kt1[128:, 1024:] = flag
    row = lax.broadcasted_iota(jnp.int32, (128, 128), 0)
    key = lax.broadcasted_iota(jnp.int32, (128, 128), 1)
    bias[...] = jnp.where(key >= row, -1e30, 0.0).astype(BF16)
    for step in range(1, 8):
        @pl.when(step > c)
        def _():
            for g in range(4):
                for kind in range(2):
                    kv[g, kind, 8 + step] = jnp.zeros((128, 128), BF16)

        @pl.when(c + step > 7)
        def _():
            for g in range(4):
                back[g, step - 1] = jnp.zeros((2, 128, 128), BF16)

    q_load.wait()
    g_load.wait()
    live = lax.broadcasted_iota(jnp.int32, (128, 128), 0) + c * 128 < len_ref[0]
    for t in range(32):
        cols = pl.ds(t * 128, 128)
        gm[:, cols] = jnp.where(live, gm[:, cols].astype(F32), 0.0).astype(BF16)

    def load_head(g):
        for t in range(16):
            rows = pl.ds(t * 128, 128)
            KT[g % 2][0:128, rows] = kv[g, 0, t].T
            VT[g % 2][:, rows] = kv[g, 1, t].T

    def load_queries(g):
        for t in range(8):
            cols = pl.ds((g * 8 + t) * 128, 128)
            qst[:, pl.ds(t * 128, 128)] = q[:, cols].T
            gst[:, pl.ds(t * 128, 128)] = gm[:, cols].T

    def soft_rows(buf, b, k, j):
        rows = pl.ds(j * BLOCK, BLOCK)
        s = S[buf][rows, :]
        m = jnp.max(s, axis=1, keepdims=True)
        dp = DP[buf][rows, :]
        e = jnp.exp2((s - m) * EXP2_SCALE)
        inv = 1.0 / jnp.sum(e, axis=1, keepdims=True)
        delta = jnp.sum(e * dp, axis=1, keepdims=True) * inv
        p = e * inv
        out = pl.ds(aligned(k * 128 + j * BLOCK, BLOCK), BLOCK)
        PT[b][out, :] = p.astype(BF16)
        DS[b][out, :] = (p * (dp - delta)).astype(BF16)

    def grad_keys(g, k):
        cols = pl.ds(aligned(k * 256, 256), 256)
        dkt = dot(qst[...], DS[g % 2][:, cols]) * SCALE
        term[g, 0, pl.ds(k * 2, 2)] = dkt.astype(BF16).T.reshape(2, 128, 128)

    def grad_values(g, k):
        cols = pl.ds(aligned(k * 256, 256), 256)
        dvt = dot(gst[...], PT[g % 2][:, cols])
        term[g, 1, pl.ds(k * 2, 2)] = dvt.astype(BF16).T.reshape(2, 128, 128)

    def grad_query(g, k):
        rows = pl.ds(aligned(k * 128, 128), 128)
        val = dot(DS[g % 2][rows, :], kv[g, 0].reshape(2048, 128)) * SCALE
        dq[:, pl.ds(aligned((g * 8 + k) * 128, 128), 128)] = val.astype(BF16)

    def unit(soft=None, ahead=None, grads=None):
        steps = 128 // BLOCK
        if ahead is not None:
            g, k, buf = ahead
            cols = pl.ds(aligned((g * 8 + k) * 128, 128), 128)
            qb, gb = q[:, cols], gm[:, cols]
            qx = jnp.concatenate([qb, bias[...]], axis=1)
            kt, vt = KT[g % 2], VT[g % 2]
        for j in range(steps):
            if ahead is not None:
                cols = pl.ds(j * 256, 256)
                if j < 4:
                    S[buf][:, cols] = dot(qb, kt[0:128, cols])
                else:
                    S[buf][:, cols] = dot(qx, kt[:, cols])
                DP[buf][:, cols] = dot(gb, vt[:, cols])
            if soft is not None:
                soft_rows(*soft, j)
            if grads is not None:
                if j == 0:
                    grad_keys(*grads)
                if j == 2:
                    grad_values(*grads)
                if j == 5:
                    grad_query(*grads)

    def back_copy(g, step):
        return pltpu.make_async_remote_copy(
            src_ref=term.at[g, :, 8 + step], dst_ref=back.at[g, step - 1],
            send_sem=d_send.at[g, step], recv_sem=d_recv.at[g, step],
            device_id=(c - step, r), device_id_type=MESH,
        )

    def send_back(g):
        for step in range(1, 8):
            @pl.when(step <= c)
            def _():
                back_copy(g, step).start()

    def finish_back(g):
        for step in range(1, 8):
            @pl.when(c + step < 8)
            def _():
                wait_bytes(back.at[g, step - 1], d_recv.at[g, step])
        cols = pl.ds(g * 128, 128)
        for kind, ref in ((0, drk_ref), (1, drv_ref)):
            total = term[g, kind, 8].astype(F32)
            for step in range(1, 8):
                total = total + back[g, step - 1, kind].astype(F32)
            ref[:, cols] = total.astype(BF16)

    def half_copy(g):
        return pltpu.make_async_remote_copy(
            src_ref=term.at[g, :, pl.ds(0, 8), other_half], dst_ref=half_in.at[g],
            send_sem=h_send.at[g], recv_sem=h_recv.at[g], device_id=sibling, device_id_type=MESH,
        )

    def z_copy(g, step):
        to_z = (z + step) % 4
        return pltpu.make_async_remote_copy(
            src_ref=half_sum.at[g, :, :, to_z], dst_ref=z_in.at[g, step - 1],
            send_sem=z_send.at[g, step], recv_sem=z_recv.at[g, step],
            device_id=(c, to_z * 4 + y_hi * 2 + core), device_id_type=MESH,
        )

    def add_halves(g):
        wait_bytes(half_in.at[g], h_recv.at[g])
        for kind in range(2):
            total = term[g, kind, pl.ds(0, 8), my_half, :].astype(F32) + half_in[g, kind].astype(F32)
            half_sum[g, kind] = total.astype(BF16).reshape(8, 4, 16, 128)
        for step in range(1, 4):
            z_copy(g, step).start()

    def add_z(g):
        for step in range(1, 4):
            wait_bytes(z_in.at[g, step - 1], z_recv.at[g, step])
        total = half_sum[g, :, :, z].astype(F32)
        for step in range(1, 4):
            total = total + z_in[g, step - 1].astype(F32)
        for cc in range(8):
            for yy in range(2):
                rows = slice(yy * 8, yy * 8 + 8)
                tile = jnp.concatenate([total[0, cc, rows], total[1, cc, rows]], axis=0)
                plane_out[cc, yy, g] = tile.astype(BF16)

    def plane_copy(step, heads, turn):
        to_c, to_y = plane_device(step)
        return pltpu.make_async_remote_copy(
            src_ref=plane_out.at[to_c, to_y, heads], dst_ref=plane_in.at[plane_id, heads],
            send_sem=x_send.at[turn], recv_sem=x_recv.at[turn],
            device_id=(to_c, z * 4 + to_y * 2 + core), device_id_type=MESH,
        )

    def plane_send(first, count, turn):
        heads = pl.ds(first, count)
        for step in range(1, 16):
            plane_copy(step, heads, turn).start()
        plane_in[plane_id, heads] = plane_out[c, y_hi, heads]

    def plane_finish(first, count, turn):
        for sem in (x_recv, x_send):
            wait_bytes(plane_in.at[pl.ds(0, 15), pl.ds(first, count)], sem.at[turn])
        for g in range(first, first + count):
            total = jnp.zeros((16, 128), F32)
            for i in range(16):
                total = total + plane_in[i, g].astype(F32)
            cols = pl.ds(g * 128, 128)
            dpk_ref[:, cols] = total[0:8].astype(BF16)
            dpv_ref[:, cols] = total[8:16].astype(BF16)

    def out_copy(g):
        cols = pl.ds(g * 1024, 1024)
        return pltpu.make_async_copy(dq.at[:, cols], dq_hbm.at[:, cols], out_sem.at[g])

    forward_head(0)
    await_head(0)
    load_head(0)
    send_head(1)
    unit(ahead=(0, 0, 0))
    for g in range(4):
        b = g % 2
        if g > 0:
            load_queries(g - 1)

        def grads_of(k):
            return None if g == 0 else (g - 1, k)

        def pair(i, _):
            @pl.when(i == 1)
            def _():
                if g < 3:
                    forward_head(g + 1)
                if g >= 2:
                    add_halves(g - 2)

            k = 2 * i
            unit(soft=(0, b, k), ahead=(g, k + 1, 1), grads=grads_of(k))
            unit(soft=(1, b, k + 1), ahead=(g, k + 2, 0), grads=grads_of(k + 1))
            return 0

        lax.fori_loop(0, 3, pair, 0)
        unit(soft=(0, b, 6), ahead=(g, 7, 1), grads=grads_of(6))
        if g < 3:
            await_head(g + 1)
            load_head(g + 1)
            unit(soft=(1, b, 7), ahead=(g + 1, 0, 0), grads=grads_of(7))
            if g < 2:
                send_head(g + 2)
        else:
            unit(soft=(1, b, 7), grads=grads_of(7))
        if g >= 1:
            send_back(g - 1)
            half_copy(g - 1).start()
            out_copy(g - 1).start()
        if g >= 2:
            add_z(g - 2)

    load_queries(3)

    def prompt_part(k, _):
        grad_keys(3, k)
        grad_values(3, k)
        return 0

    lax.fori_loop(4, 8, prompt_part, 0)
    send_back(3)
    lax.fori_loop(0, 4, prompt_part, 0)
    half_copy(3).start()
    add_halves(2)

    def query_part(k, _):
        grad_query(3, k)
        return 0

    lax.fori_loop(0, 4, query_part, 0)
    add_halves(3)
    lax.fori_loop(4, 8, query_part, 0)
    out_copy(3).start()
    add_z(2)
    plane_send(0, 3, 0)
    for g in range(3):
        finish_back(g)
    add_z(3)
    plane_send(3, 1, 1)
    finish_back(3)
    plane_finish(0, 3, 0)
    plane_finish(3, 1, 1)

    for g in range(4):
        wait_bytes(kv.at[g, :, pl.ds(0, 7), my_half], p_send.at[g])
        wait_bytes(kv.at[g, :, pl.ds(0, 8), my_half], f_send.at[g])
        wait_bytes(half_in.at[g], h_send.at[g])
        for step in range(1, 8):
            @pl.when(c + step < 8)
            def _():
                wait_bytes(kv.at[g, :, 8], r_send.at[g, step])

            @pl.when(step <= c)
            def _():
                wait_bytes(term.at[g, :, 8 + step], d_send.at[g, step])
        for step in range(1, 4):
            wait_bytes(z_in.at[g, step - 1], z_send.at[g, step])
        out_copy(g).wait()


def per_device(query, prompt_keys, prompt_value_rows, response_keys, response_values, d_out, lengths):
    any_spec = pl.BlockSpec(memory_space=pl.ANY)
    vmem = pl.BlockSpec(memory_space=pltpu.VMEM)
    dma = pltpu.SemaphoreType.DMA
    scratch = [
        pltpu.VMEM((128, 4096), BF16),
        pltpu.VMEM((128, 4096), BF16),
        pltpu.VMEM((128, 4096), BF16),
        pltpu.VMEM((2, 128, 512), BF16),
        pltpu.VMEM((4, 2, 16, 128, 128), BF16),
        pltpu.VMEM((4, 2, 16, 128, 128), BF16),
        pltpu.VMEM((4, 7, 2, 128, 128), BF16),
        pltpu.VMEM((4, 2, 8, 64, 128), BF16),
        pltpu.VMEM((4, 2, 8, 4, 16, 128), BF16),
        pltpu.VMEM((4, 3, 2, 8, 16, 128), BF16),
        pltpu.VMEM((8, 2, 4, 16, 128), BF16),
        pltpu.VMEM((16, 4, 16, 128), BF16),
    ]
    scratch += [pltpu.VMEM((1024, 2048), BF16)] * 4
    scratch += [pltpu.VMEM((128, 2048), F32)] * 4
    scratch += [pltpu.VMEM((256, 2048), BF16)] * 2 + [pltpu.VMEM((128, 2048), BF16)] * 2
    scratch += [pltpu.VMEM((128, 1024), BF16)] * 2 + [pltpu.VMEM((128, 128), BF16)]
    scratch += [dma((12,)), dma((4,)), dma((4,)), dma((4,)), dma((4,)), dma((4,))]
    scratch += [dma((4, 8))] * 4 + [dma((4,))] * 2 + [dma((4, 4))] * 2 + [dma((2,))] * 2
    out = pl.pallas_call(
        kernel,
        out_shape=[
            jax.ShapeDtypeStruct((128, 4096), BF16),
            jax.ShapeDtypeStruct((128, 512), BF16),
            jax.ShapeDtypeStruct((128, 512), BF16),
            jax.ShapeDtypeStruct((8, 512), BF16),
            jax.ShapeDtypeStruct((8, 512), BF16),
        ],
        in_specs=[any_spec] * 6 + [pl.BlockSpec(memory_space=pltpu.SMEM)],
        out_specs=[any_spec] + [vmem] * 4,
        scratch_shapes=scratch,
        compiler_params=pltpu.CompilerParams(
            collective_id=0, has_side_effects=True, vmem_limit_bytes=58 * 2**20
        ),
    )(query[0], prompt_keys, prompt_value_rows, response_keys[0], response_values[0], d_out[0], lengths)
    d_query, d_rk, d_rv, d_pk, d_pv = out
    return d_query[None], d_rk[None], d_rv[None], d_pk, d_pv


def solution(mesh):
    return jax.shard_map(
        per_device,
        mesh=mesh,
        in_specs=(
            P("resp", "ctx", None),
            P("ctx", None),
            P("ctx", None),
            P("resp", "ctx", None),
            P("resp", "ctx", None),
            P("resp", "ctx", None),
            P("resp"),
        ),
        out_specs=(
            P("resp", "ctx", None),
            P("resp", "ctx", None),
            P("resp", "ctx", None),
            P(("ctx", "resp"), None),
            P(("ctx", "resp"), None),
        ),
        check_vma=False,
    )
```

```python
import functools

import jax
import jax.numpy as jnp
from jax import lax
from jax.experimental import pallas as pl
from jax.experimental.pallas import tpu as pltpu
from jax.sharding import PartitionSpec as P

F32, BF16 = jnp.float32, jnp.bfloat16
MESH = pl.DeviceIdType.MESH
SCALE = 128 ** -0.5
EXP2_SCALE = SCALE * 1.4426950408889634
BLOCK = 16
KEY_ORDER = (4, 6, 0, 2)


def dot(a, b):
    return lax.dot_general(a, b, (((1,), (0,)), ((), ())), preferred_element_type=F32)


def aligned(x, n):
    return x if isinstance(x, int) else pl.multiple_of(x, n)


def wait_bytes(ref, sem):
    pltpu.make_async_copy(ref, ref, sem).wait()


def kernel(
    q_hbm, pk_hbm, pv_hbm, rk_hbm, rv_hbm, g_hbm, len_ref,
    dq_hbm, drk_ref, drv_ref, dpk_ref, dpv_ref,
    q, gm, dq, pstage, pwide, kv, term, back, half_in, half_sum, z_in, plane_out, plane_in,
    pt0, pt1, ds0, ds1, s0, s1, dp0, dp1, kt0, kt1, vt0, vt1, qst0, qst1, gst0, gst1, bias,
    loc_sem, out_sem, p_send, p_recv, a_send, a_recv, f_send, f_recv, r_send, r_recv, d_send, d_recv,
    h_send, h_recv, z_send, z_recv, x_send, x_recv,
):
    c, r = lax.axis_index("ctx"), lax.axis_index("resp")
    y_lo, x = c // 4, c % 4
    z, y_hi, core = r // 4, (r // 2) % 2, r % 2
    sibling = (c, z * 4 + y_hi * 2 + 1 - core)
    other = 1 - core
    PT, DS, KT, VT, S, DP = [pt0, pt1], [ds0, ds1], [kt0, kt1], [vt0, vt1], [s0, s1], [dp0, dp1]
    QT, GT = [qst0, qst1], [gst0, gst1]

    loads = []
    for g in range(4):
        cols = pl.ds(g * 128, 128)
        loads.append(pltpu.make_async_copy(rk_hbm.at[:, cols], kv.at[g, 0, 8], loc_sem.at[len(loads)]))
        loads.append(pltpu.make_async_copy(rv_hbm.at[:, cols], kv.at[g, 1, 8], loc_sem.at[len(loads)]))
    loads.append(pltpu.make_async_copy(pk_hbm, pstage.at[0], loc_sem.at[8]))
    loads.append(pltpu.make_async_copy(pv_hbm, pstage.at[1], loc_sem.at[9]))
    q_load = pltpu.make_async_copy(q_hbm, q, loc_sem.at[10])
    g_load = pltpu.make_async_copy(g_hbm, gm, loc_sem.at[11])
    for copy in loads:
        copy.start()
    q_load.start()
    g_load.start()

    barrier = pltpu.get_barrier_semaphore()
    plane_id = c * 2 + y_hi

    def plane_device(step):
        to = (plane_id + step) % 16
        return to // 2, to % 2

    for step in range(1, 16):
        to_c, to_y = plane_device(step)
        pl.semaphore_signal(barrier, inc=1, device_id=(to_c, z * 4 + to_y * 2 + core), device_id_type=MESH)
    for step in range(1, 4):
        to_z = (z + step) % 4
        pl.semaphore_signal(barrier, inc=1, device_id=(c, to_z * 4 + y_hi * 2 + core), device_id_type=MESH)
    pl.semaphore_signal(barrier, inc=1, device_id=sibling, device_id_type=MESH)

    my_half = pl.ds(pl.multiple_of(core * 64, 64), 64)
    other_half = pl.ds(pl.multiple_of(other * 64, 64), 64)
    my_rows = pl.ds(pl.multiple_of(core * 64 + z * 16, 16), 16)
    loads[8].wait()
    loads[9].wait()
    for kind in range(2):
        pwide[kind] = pstage[kind].astype(F32)
        parts = [pwide[kind, pl.ds(pl.multiple_of((z * 4 + yy * 2 + core) * 8, 8), 8), :] for yy in range(2)]
        mine = jnp.concatenate(parts, axis=0).astype(BF16)
        for g in range(4):
            kv[g, kind, c, my_rows, :] = mine[:, g * 128 : g * 128 + 128]
    pl.semaphore_wait(barrier, 19)

    def prompt_copy(turn, step):
        heads = pl.ds(0, 1) if turn == 0 else pl.ds(1, 3)
        to_c = (c + step) % 8
        to_y = jnp.where(to_c // 4 == y_lo, y_hi, 1 - y_hi)
        return pltpu.make_async_remote_copy(
            src_ref=kv.at[heads, :, c, my_rows], dst_ref=kv.at[heads, :, c, my_rows],
            send_sem=p_send.at[turn], recv_sem=p_recv.at[turn],
            device_id=(to_c, z * 4 + to_y * 2 + core), device_id_type=MESH,
        )

    def prompt_bytes(turn):
        heads = pl.ds(0, 1) if turn == 0 else pl.ds(1, 3)
        return kv.at[heads, :, pl.ds(0, 7), pl.ds(0, 16)]

    def column_copy(g, step):
        to_z = (z + step) % 4
        return pltpu.make_async_remote_copy(
            src_ref=kv.at[g, :, pl.ds(0, 8), my_rows], dst_ref=kv.at[g, :, pl.ds(0, 8), my_rows],
            send_sem=a_send.at[g], recv_sem=a_recv.at[g],
            device_id=(c, to_z * 4 + y_hi * 2 + core), device_id_type=MESH,
        )

    def column_bytes(g):
        return kv.at[g, :, pl.ds(0, 8), pl.ds(0, 48)]

    def forward_copy(g):
        return pltpu.make_async_remote_copy(
            src_ref=kv.at[g, :, pl.ds(0, 8), my_half], dst_ref=kv.at[g, :, pl.ds(0, 8), my_half],
            send_sem=f_send.at[g], recv_sem=f_recv.at[g], device_id=sibling, device_id_type=MESH,
        )

    def resp_copy(g, step):
        return pltpu.make_async_remote_copy(
            src_ref=kv.at[g, :, 8], dst_ref=kv.at[g, :, 8 + step],
            send_sem=r_send.at[g, step], recv_sem=r_recv.at[g, step],
            device_id=(c + step, r), device_id_type=MESH,
        )

    def send_prompt(turn):
        for step in range(1, 8):
            prompt_copy(turn, step).start()

    def send_column(g):
        for step in range(1, 4):
            column_copy(g, step).start()

    def forward_head(g):
        wait_bytes(column_bytes(g), a_recv.at[g])
        forward_copy(g).start()

    def send_resp(g):
        for step in range(1, 8):
            @pl.when(c + step < 8)
            def _():
                resp_copy(g, step).start()

    def await_head(g):
        for step in range(1, 8):
            @pl.when(step <= c)
            def _():
                wait_bytes(kv.at[g, :, 8 + step], r_recv.at[g, step])
        wait_bytes(kv.at[g, :, pl.ds(0, 8), other_half], f_recv.at[g])

    send_prompt(0)
    for copy in loads[:8]:
        copy.wait()
    send_resp(0)

    row = lax.broadcasted_iota(jnp.int32, (128, 1024), 0)
    key = lax.broadcasted_iota(jnp.int32, (128, 1024), 1)
    flag = ((key == row + 1) & (key < 128)) | ((row == 127) & (key >= (c + 1) * 128))
    flag = jnp.where(flag, 1.0, 0.0).astype(BF16)
    kt0[128:, 1024:] = flag
    kt1[128:, 1024:] = flag
    row = lax.broadcasted_iota(jnp.int32, (128, 128), 0)
    key = lax.broadcasted_iota(jnp.int32, (128, 128), 1)
    bias[...] = jnp.where(key >= row, -1e30, 0.0).astype(BF16)
    for step in range(1, 8):
        @pl.when(step > c)
        def _():
            for g in range(4):
                for kind in range(2):
                    kv[g, kind, 8 + step] = jnp.zeros((128, 128), BF16)

        @pl.when(c + step > 7)
        def _():
            for g in range(4):
                back[g, step - 1] = jnp.zeros((2, 128, 128), BF16)

    q_load.wait()
    g_load.wait()
    live = lax.broadcasted_iota(jnp.int32, (128, 128), 0) + c * 128 < len_ref[0]
    for t in range(32):
        cols = pl.ds(t * 128, 128)
        gm[:, cols] = jnp.where(live, gm[:, cols].astype(F32), 0.0).astype(BF16)

    def load_block(g, t):
        rows = pl.ds(t * 128, 128)
        KT[g % 2][0:128, rows] = kv[g, 0, t].T
        VT[g % 2][:, rows] = kv[g, 1, t].T

    def load_query(g, k):
        cols = pl.ds((g * 8 + k) * 128, 128)
        QT[g % 2][:, pl.ds(k * 128, 128)] = q[:, cols].T
        GT[g % 2][:, pl.ds(k * 128, 128)] = gm[:, cols].T

    def soft_rows(buf, b, k, j):
        rows = pl.ds(j * BLOCK, BLOCK)
        s = S[buf][rows, :]
        m = jnp.max(s, axis=1, keepdims=True)
        dp = DP[buf][rows, :]
        e = jnp.exp2((s - m) * EXP2_SCALE)
        inv = 1.0 / jnp.sum(e, axis=1, keepdims=True)
        delta = jnp.sum(e * dp, axis=1, keepdims=True) * inv
        p = e * inv
        out = pl.ds(aligned(k * 128 + j * BLOCK, BLOCK), BLOCK)
        PT[b][out, :] = p.astype(BF16)
        DS[b][out, :] = (p * (dp - delta)).astype(BF16)

    def grad_keys(g, k, kind):
        cols = pl.ds(k * 256, 512)
        if kind == 0:
            val = dot(QT[g % 2][...], DS[g % 2][:, cols]) * SCALE
        else:
            val = dot(GT[g % 2][...], PT[g % 2][:, cols])
        term[g, kind, pl.ds(k * 2, 4)] = val.astype(BF16).T.reshape(4, 128, 128)

    def grad_query(g, k):
        rows = pl.ds(aligned(k * 128, 128), 128)
        val = dot(DS[g % 2][rows, :], kv[g, 0].reshape(2048, 128)) * SCALE
        dq[:, pl.ds(aligned((g * 8 + k) * 128, 128), 128)] = val.astype(BF16)

    def unit(soft=None, ahead=None, grads=None, load=None):
        steps = 128 // BLOCK
        if ahead is not None:
            g, k = ahead
            cols = pl.ds((g * 8 + k) * 128, 128)
            qb, gb = q[:, cols], gm[:, cols]
            qx = jnp.concatenate([qb, bias[...]], axis=1)
            kt, vt = KT[g % 2], VT[g % 2]
            s_ref, dp_ref = S[k % 2], DP[k % 2]
        for j in range(steps):
            if load is not None:
                for t in range(2 * j, 2 * j + 2):
                    load_block(load, t)
            if ahead is not None:
                cols = pl.ds(j * 256, 256)
                if j < 4:
                    s_ref[:, cols] = dot(qb, kt[0:128, cols])
                else:
                    s_ref[:, cols] = dot(qx, kt[:, cols])
                dp_ref[:, cols] = dot(gb, vt[:, cols])
            if soft is not None:
                soft_rows(soft[1] % 2, soft[0] % 2, soft[1], j)
            if grads is not None:
                g1, k1 = grads
                if k1 < 4 and j in (0, 4):
                    grad_keys(g1, KEY_ORDER[k1], j // 4)
                if k1 >= 4 and j in (0, 4):
                    grad_query(g1, 2 * (k1 - 4) + j // 4)
            if soft is not None and j == 6:
                load_query(*soft)

    def back_copy(g, step):
        return pltpu.make_async_remote_copy(
            src_ref=term.at[g, :, 8 + step], dst_ref=back.at[g, step - 1],
            send_sem=d_send.at[g, step], recv_sem=d_recv.at[g, step],
            device_id=(c - step, r), device_id_type=MESH,
        )

    def send_back(g):
        for step in range(1, 8):
            @pl.when(step <= c)
            def _():
                back_copy(g, step).start()

    def finish_back(g):
        for step in range(1, 8):
            @pl.when(c + step < 8)
            def _():
                wait_bytes(back.at[g, step - 1], d_recv.at[g, step])
        cols = pl.ds(g * 128, 128)
        for kind, ref in ((0, drk_ref), (1, drv_ref)):
            total = term[g, kind, 8].astype(F32)
            for step in range(1, 8):
                total = total + back[g, step - 1, kind].astype(F32)
            ref[:, cols] = total.astype(BF16)

    def half_copy(g):
        return pltpu.make_async_remote_copy(
            src_ref=term.at[g, :, pl.ds(0, 8), other_half], dst_ref=half_in.at[g],
            send_sem=h_send.at[g], recv_sem=h_recv.at[g], device_id=sibling, device_id_type=MESH,
        )

    def z_copy(g, step):
        to_z = (z + step) % 4
        return pltpu.make_async_remote_copy(
            src_ref=half_sum.at[g, :, :, to_z], dst_ref=z_in.at[g, step - 1],
            send_sem=z_send.at[g, step], recv_sem=z_recv.at[g, step],
            device_id=(c, to_z * 4 + y_hi * 2 + core), device_id_type=MESH,
        )

    def add_halves(g):
        wait_bytes(half_in.at[g], h_recv.at[g])
        for kind in range(2):
            total = term[g, kind, pl.ds(0, 8), my_half, :].astype(F32) + half_in[g, kind].astype(F32)
            half_sum[g, kind] = total.astype(BF16).reshape(8, 4, 16, 128)
        for step in range(1, 4):
            z_copy(g, step).start()

    def add_z(g):
        for step in range(1, 4):
            wait_bytes(z_in.at[g, step - 1], z_recv.at[g, step])
        total = half_sum[g, :, :, z].astype(F32)
        for step in range(1, 4):
            total = total + z_in[g, step - 1].astype(F32)
        for cc in range(8):
            for yy in range(2):
                rows = slice(yy * 8, yy * 8 + 8)
                tile = jnp.concatenate([total[0, cc, rows], total[1, cc, rows]], axis=0)
                plane_out[cc, yy, g] = tile.astype(BF16)

    def plane_copy(step, heads, turn):
        to_c, to_y = plane_device(step)
        return pltpu.make_async_remote_copy(
            src_ref=plane_out.at[to_c, to_y, heads], dst_ref=plane_in.at[plane_id, heads],
            send_sem=x_send.at[turn], recv_sem=x_recv.at[turn],
            device_id=(to_c, z * 4 + to_y * 2 + core), device_id_type=MESH,
        )

    def plane_send(first, count, turn):
        heads = pl.ds(first, count)
        for step in range(1, 16):
            plane_copy(step, heads, turn).start()
        plane_in[plane_id, heads] = plane_out[c, y_hi, heads]

    def plane_finish(first, count, turn):
        for sem in (x_recv, x_send):
            wait_bytes(plane_in.at[pl.ds(0, 15), pl.ds(first, count)], sem.at[turn])
        for g in range(first, first + count):
            total = jnp.zeros((16, 128), F32)
            for i in range(16):
                total = total + plane_in[i, g].astype(F32)
            cols = pl.ds(g * 128, 128)
            dpk_ref[:, cols] = total[0:8].astype(BF16)
            dpv_ref[:, cols] = total[8:16].astype(BF16)

    def out_copy(g):
        cols = pl.ds(g * 1024, 1024)
        return pltpu.make_async_copy(dq.at[:, cols], dq_hbm.at[:, cols], out_sem.at[g])

    wait_bytes(prompt_bytes(0), p_recv.at[0])
    send_column(0)
    send_prompt(1)
    forward_head(0)
    send_resp(1)
    wait_bytes(prompt_bytes(1), p_recv.at[1])
    send_column(1)
    await_head(0)
    send_resp(2)
    send_column(2)
    for t in range(16):
        load_block(0, t)
    unit(ahead=(0, 0))
    for g in range(4):
        for k in range(8):
            if k == 2:
                if g < 3:
                    forward_head(g + 1)
                if g >= 1:
                    send_back(g - 1)
                if g >= 2:
                    add_z(g - 2)
            if k == 4 and g >= 1:
                half_copy(g - 1).start()
            if k == 6:
                if g < 3:
                    await_head(g + 1)
                if g == 0:
                    send_resp(3)
                    send_column(3)
                if g >= 1:
                    add_halves(g - 1)
            ahead = (g, k + 1) if k < 7 else (g + 1, 0) if g < 3 else None
            unit(
                soft=(g, k), ahead=ahead, grads=(g - 1, k) if g > 0 else None,
                load=g + 1 if k == 6 and g < 3 else None,
            )
        if g >= 1:
            out_copy(g - 1).start()

    for k in KEY_ORDER[2:]:
        grad_keys(3, k, 0)
        grad_keys(3, k, 1)
    half_copy(3).start()
    for k in KEY_ORDER[:2]:
        grad_keys(3, k, 0)
        grad_keys(3, k, 1)
    send_back(3)
    add_halves(3)
    add_z(2)
    plane_send(0, 3, 0)
    for k in range(4):
        grad_query(3, k)
    for k in range(4, 8):
        grad_query(3, k)
    out_copy(3).start()
    add_z(3)
    plane_send(3, 1, 1)
    for g in range(3):
        finish_back(g)
    plane_finish(0, 3, 0)
    finish_back(3)
    plane_finish(3, 1, 1)

    for turn in range(2):
        wait_bytes(prompt_bytes(turn), p_send.at[turn])
    for g in range(4):
        wait_bytes(column_bytes(g), a_send.at[g])
        wait_bytes(kv.at[g, :, pl.ds(0, 8), my_half], f_send.at[g])
        wait_bytes(half_in.at[g], h_send.at[g])
        for step in range(1, 8):
            @pl.when(c + step < 8)
            def _():
                wait_bytes(kv.at[g, :, 8], r_send.at[g, step])

            @pl.when(step <= c)
            def _():
                wait_bytes(term.at[g, :, 8 + step], d_send.at[g, step])
        for step in range(1, 4):
            wait_bytes(z_in.at[g, step - 1], z_send.at[g, step])
        out_copy(g).wait()


def hand_over(*refs):
    ins, outs, bufs, in_sem, out_sem = refs[:5], refs[5:10], refs[10:15], refs[15], refs[16]
    quarters = [(0, pl.ds(i * 1024, 1024)) for i in range(4)]
    parts = quarters + [(i, pl.ds(0, 512)) for i in range(1, 5)]
    reads = [
        pltpu.make_async_copy(ins[i].at[:, cols], bufs[i].at[:, cols], in_sem.at[n])
        for n, (i, cols) in enumerate(parts)
    ]
    writes = [
        pltpu.make_async_copy(bufs[i].at[:, cols], outs[i].at[:, cols], out_sem.at[n])
        for n, (i, cols) in enumerate(parts)
    ]
    for copy in reads:
        copy.start()
    for read, write in zip(reads, writes):
        read.wait()
        write.start()
    for copy in writes:
        copy.wait()


def per_device(query, prompt_keys, prompt_value_rows, response_keys, response_values, d_out, lengths):
    any_spec = pl.BlockSpec(memory_space=pl.ANY)
    vmem = pl.BlockSpec(memory_space=pltpu.VMEM)
    dma = pltpu.SemaphoreType.DMA
    scratch = [
        pltpu.VMEM((128, 4096), BF16),
        pltpu.VMEM((128, 4096), BF16),
        pltpu.VMEM((128, 4096), BF16),
        pltpu.VMEM((2, 128, 512), BF16),
        pltpu.VMEM((2, 128, 512), F32),
        pltpu.VMEM((4, 2, 16, 128, 128), BF16),
        pltpu.VMEM((4, 2, 16, 128, 128), BF16),
        pltpu.VMEM((4, 7, 2, 128, 128), BF16),
        pltpu.VMEM((4, 2, 8, 64, 128), BF16),
        pltpu.VMEM((4, 2, 8, 4, 16, 128), BF16),
        pltpu.VMEM((4, 3, 2, 8, 16, 128), BF16),
        pltpu.VMEM((8, 2, 4, 16, 128), BF16),
        pltpu.VMEM((16, 4, 16, 128), BF16),
    ]
    scratch += [pltpu.VMEM((1024, 2048), BF16)] * 4
    scratch += [pltpu.VMEM((128, 2048), F32)] * 4
    scratch += [pltpu.VMEM((256, 2048), BF16)] * 2 + [pltpu.VMEM((128, 2048), BF16)] * 2
    scratch += [pltpu.VMEM((128, 1024), BF16)] * 4 + [pltpu.VMEM((128, 128), BF16)]
    scratch += [dma((12,)), dma((4,)), dma((2,)), dma((2,)), dma((4,)), dma((4,)), dma((4,)), dma((4,))]
    scratch += [dma((4, 8))] * 4 + [dma((4,))] * 2 + [dma((4, 4))] * 2 + [dma((2,))] * 2
    out = pl.pallas_call(
        kernel,
        out_shape=[
            jax.ShapeDtypeStruct((128, 4096), BF16),
            jax.ShapeDtypeStruct((128, 512), BF16),
            jax.ShapeDtypeStruct((128, 512), BF16),
            jax.ShapeDtypeStruct((8, 512), BF16),
            jax.ShapeDtypeStruct((8, 512), BF16),
        ],
        in_specs=[any_spec] * 6 + [pl.BlockSpec(memory_space=pltpu.SMEM)],
        out_specs=[any_spec] + [vmem] * 4,
        scratch_shapes=scratch,
        compiler_params=pltpu.CompilerParams(
            collective_id=0, has_side_effects=True, vmem_limit_bytes=62 * 2**20
        ),
    )(query[0], prompt_keys, prompt_value_rows, response_keys[0], response_values[0], d_out[0], lengths)
    d_query, d_rk, d_rv, d_pk, d_pv = pl.pallas_call(
        hand_over,
        out_shape=[jax.ShapeDtypeStruct(a.shape, a.dtype) for a in out],
        in_specs=[any_spec] * 5,
        out_specs=[any_spec] * 5,
        scratch_shapes=[pltpu.VMEM(a.shape, a.dtype) for a in out] + [dma((8,)), dma((8,))],
    )(*out)
    return d_query[None], d_rk[None], d_rv[None], d_pk, d_pv


def solution(mesh):
    return jax.shard_map(
        per_device,
        mesh=mesh,
        in_specs=(
            P("resp", "ctx", None),
            P("ctx", None),
            P("ctx", None),
            P("resp", "ctx", None),
            P("resp", "ctx", None),
            P("resp", "ctx", None),
            P("resp"),
        ),
        out_specs=(
            P("resp", "ctx", None),
            P("resp", "ctx", None),
            P("resp", "ctx", None),
            P(("ctx", "resp"), None),
            P(("ctx", "resp"), None),
        ),
        check_vma=False,
    )
```

```python
import functools

import jax
import jax.numpy as jnp
from jax import lax
from jax.experimental import pallas as pl
from jax.experimental.pallas import tpu as pltpu
from jax.sharding import PartitionSpec as P

F32, BF16 = jnp.float32, jnp.bfloat16
MESH = pl.DeviceIdType.MESH
SCALE = 128 ** -0.5
EXP2_SCALE = SCALE * 1.4426950408889634
BLOCK = 16
RELAY_AT = {(0, 2): 2, (1, 1): 3}
ROWS = 256


def dot(a, b):
    return lax.dot_general(a, b, (((1,), (0,)), ((), ())), preferred_element_type=F32)


def aligned(x, n):
    return x if isinstance(x, int) else pl.multiple_of(x, n)


def wait_bytes(ref, sem):
    pltpu.make_async_copy(ref, ref, sem).wait()


def kernel(
    q_hbm, pk_hbm, pv_hbm, rk_hbm, rv_hbm, g_hbm, len_ref,
    dq_hbm, drk_ref, drv_ref, dpk_ref, dpv_ref,
    q, gm, dq, pstage, pwide, kv, term, back, half_in, half_sum, z_in, plane_out, plane_in,
    pt0, pt1, ds0, ds1, s0, s1, dp0, dp1, kt0, kt1, vt0, vt1, qst0, qst1, gst0, gst1, bias,
    loc_sem, out_sem, p_send, p_recv, a_send, a_recv, f_send, f_recv, r_send, r_recv, d_send, d_recv,
    h_send, h_recv, z_send, z_recv, x_send, x_recv, y_send,
):
    c, r = lax.axis_index("ctx"), lax.axis_index("resp")
    y_lo, x = c // 4, c % 4
    z, y_hi, core = r // 4, (r // 2) % 2, r % 2
    sibling = (c, z * 4 + y_hi * 2 + 1 - core)
    other = 1 - core
    PT, DS, KT, VT, S, DP = [pt0, pt1], [ds0, ds1], [kt0, kt1], [vt0, vt1], [s0, s1], [dp0, dp1]
    QT, GT = [qst0, qst1], [gst0, gst1]

    loads = []
    for g in range(4):
        cols = pl.ds(g * 128, 128)
        loads.append(pltpu.make_async_copy(rk_hbm.at[:, cols], kv.at[g, 0, 8], loc_sem.at[len(loads)]))
        loads.append(pltpu.make_async_copy(rv_hbm.at[:, cols], kv.at[g, 1, 8], loc_sem.at[len(loads)]))
    loads.append(pltpu.make_async_copy(pk_hbm, pstage.at[0], loc_sem.at[8]))
    loads.append(pltpu.make_async_copy(pv_hbm, pstage.at[1], loc_sem.at[9]))
    q_load = pltpu.make_async_copy(q_hbm, q, loc_sem.at[10])
    g_load = pltpu.make_async_copy(g_hbm, gm, loc_sem.at[11])
    for copy in loads[8:] + loads[:8]:
        copy.start()
    q_load.start()
    g_load.start()

    barrier = pltpu.get_barrier_semaphore()
    plane_id = c * 2 + y_hi

    def plane_device(step):
        to = (plane_id + step) % 16
        return to // 2, to % 2

    for step in range(1, 16):
        to_c, to_y = plane_device(step)
        pl.semaphore_signal(barrier, inc=1, device_id=(to_c, z * 4 + to_y * 2 + core), device_id_type=MESH)
    for step in range(1, 4):
        to_z = (z + step) % 4
        pl.semaphore_signal(barrier, inc=1, device_id=(c, to_z * 4 + y_hi * 2 + core), device_id_type=MESH)
    pl.semaphore_signal(barrier, inc=1, device_id=sibling, device_id_type=MESH)

    my_half = pl.ds(pl.multiple_of(core * 64, 64), 64)
    other_half = pl.ds(pl.multiple_of(other * 64, 64), 64)
    my_rows = pl.ds(pl.multiple_of(core * 64 + z * 16, 16), 16)
    far_z = (z + 2) % 4
    far_rows = pl.ds(pl.multiple_of(core * 64 + far_z * 16, 16), 16)
    loads[8].wait()
    loads[9].wait()
    for kind in range(2):
        pwide[kind] = pstage[kind].astype(F32)
        for zz, rows in ((z, my_rows), (far_z, far_rows)):
            parts = [pwide[kind, pl.ds(pl.multiple_of((zz * 4 + yy * 2 + core) * 8, 8), 8), :] for yy in range(2)]
            mine = jnp.concatenate(parts, axis=0).astype(BF16)
            for g in range(4):
                kv[g, kind, c, rows, :] = mine[:, g * 128 : g * 128 + 128]
    pl.semaphore_wait(barrier, 19)

    def prompt_copy(turn, step, rows):
        heads = pl.ds(0, 1) if turn == 0 else pl.ds(1, 3)
        to_c = (c + step) % 8
        to_y = jnp.where(to_c // 4 == y_lo, y_hi, 1 - y_hi)
        return pltpu.make_async_remote_copy(
            src_ref=kv.at[heads, :, c, rows], dst_ref=kv.at[heads, :, c, rows],
            send_sem=p_send.at[turn], recv_sem=p_recv.at[turn],
            device_id=(to_c, z * 4 + to_y * 2 + core), device_id_type=MESH,
        )

    def prompt_bytes(turn):
        heads = pl.ds(0, 1) if turn == 0 else pl.ds(1, 3)
        return kv.at[heads, :, pl.ds(0, 7), pl.ds(0, 32)]

    def column_copy(g, step):
        to_z = (z + step) % 4
        return pltpu.make_async_remote_copy(
            src_ref=kv.at[g, :, pl.ds(0, 8), my_rows], dst_ref=kv.at[g, :, pl.ds(0, 8), my_rows],
            send_sem=a_send.at[g], recv_sem=a_recv.at[g],
            device_id=(c, to_z * 4 + y_hi * 2 + core), device_id_type=MESH,
        )

    def column_bytes(g):
        return kv.at[g, :, pl.ds(0, 8), pl.ds(0, 32)]

    def forward_copy(g):
        return pltpu.make_async_remote_copy(
            src_ref=kv.at[g, :, pl.ds(0, 8), my_half], dst_ref=kv.at[g, :, pl.ds(0, 8), my_half],
            send_sem=f_send.at[g], recv_sem=f_recv.at[g], device_id=sibling, device_id_type=MESH,
        )

    def resp_copy(g, step):
        return pltpu.make_async_remote_copy(
            src_ref=kv.at[g, :, 8], dst_ref=kv.at[g, :, 8 + step],
            send_sem=r_send.at[g, step], recv_sem=r_recv.at[g, step],
            device_id=(c + step, r), device_id_type=MESH,
        )

    def send_prompt(turn):
        for step in range(1, 8):
            prompt_copy(turn, step, my_rows).start()
            prompt_copy(turn, step, far_rows).start()

    def send_column(g):
        for step in (1, 3):
            column_copy(g, step).start()

    def forward_head(g):
        wait_bytes(column_bytes(g), a_recv.at[g])
        forward_copy(g).start()

    def send_resp(g):
        for step in range(1, 4):
            @pl.when(x + step < 4)
            def _():
                resp_copy(g, step).start()

        @pl.when(y_lo == 0)
        def _():
            resp_copy(g, 4).start()

    def down_copy(g, step):
        return pltpu.make_async_remote_copy(
            src_ref=kv.at[g, :, 8 + step], dst_ref=kv.at[g, :, 12 + step],
            send_sem=y_send.at[g, step], recv_sem=r_recv.at[g, 4 + step],
            device_id=(c + 4, r), device_id_type=MESH,
        )

    def side_copy(g, step):
        return pltpu.make_async_remote_copy(
            src_ref=kv.at[g, :, 12], dst_ref=kv.at[g, :, 12 - step],
            send_sem=y_send.at[g, step], recv_sem=r_recv.at[g, 4 - step],
            device_id=(c - step, r), device_id_type=MESH,
        )

    def wrap_copy(g):
        return pltpu.make_async_remote_copy(
            src_ref=kv.at[g, :, 12], dst_ref=kv.at[g, :, 15],
            send_sem=y_send.at[g, 4], recv_sem=r_recv.at[g, 7],
            device_id=(c + 3, r), device_id_type=MESH,
        )

    def relays(g, act):
        for step in range(1, 4):
            @pl.when((y_lo == 0) & (step <= x))
            def _():
                if act:
                    wait_bytes(kv.at[g, :, 8 + step], r_recv.at[g, step])

            if step < 3:
                @pl.when((y_lo == 0) & (step <= x))
                def _():
                    if act:
                        down_copy(g, step).start()
                    else:
                        wait_bytes(kv.at[g, :, 8], y_send.at[g, step])

        @pl.when(y_lo == 1)
        def _():
            if act:
                wait_bytes(kv.at[g, :, 12], r_recv.at[g, 4])

        for step in range(1, 4):
            @pl.when((y_lo == 1) & (step <= x))
            def _():
                if act:
                    side_copy(g, step).start()
                else:
                    wait_bytes(kv.at[g, :, 8], y_send.at[g, step])

        @pl.when((y_lo == 1) & (x == 0))
        def _():
            if act:
                wrap_copy(g).start()
            else:
                wait_bytes(kv.at[g, :, 8], y_send.at[g, 4])

    def await_head(g):
        for step in (1, 2, 3, 5, 6, 7):
            @pl.when((y_lo == 1) & (step <= c))
            def _():
                wait_bytes(kv.at[g, :, 8 + step], r_recv.at[g, step])
        wait_bytes(kv.at[g, :, pl.ds(0, 8), other_half], f_recv.at[g])

    send_prompt(0)
    for copy in loads[:8]:
        copy.wait()
    send_resp(0)

    def load_block(g, t):
        rows = pl.ds(t * 128, 128)
        KT[g % 2][0:128, rows] = kv[g, 0, t].T
        VT[g % 2][:, rows] = kv[g, 1, t].T

    def load_query(g, k):
        for h in range(2 * k, 2 * k + 2):
            cols = pl.ds((g * 8 + h) * 128, 128)
            QT[g % 2][:, pl.ds(h * 128, 128)] = q[:, cols].T
            GT[g % 2][:, pl.ds(h * 128, 128)] = gm[:, cols].T

    def soft_rows(buf, b, k, j):
        rows = pl.ds(j * BLOCK, BLOCK)
        s = S[buf][rows, :]
        m = jnp.max(s, axis=1, keepdims=True)
        dp = DP[buf][rows, :]
        e = jnp.exp2((s - m) * EXP2_SCALE)
        inv = 1.0 / jnp.sum(e, axis=1, keepdims=True)
        delta = jnp.sum(e * dp, axis=1, keepdims=True) * inv
        p = e * inv
        out = pl.ds(k * ROWS + j * BLOCK, BLOCK)
        PT[b][out, :] = p.astype(BF16)
        DS[b][out, :] = (p * (dp - delta)).astype(BF16)

    def grad_keys(g, k, kind):
        cols = pl.ds(k * 256, 512)
        if kind == 0:
            val = dot(QT[g % 2][...], DS[g % 2][:, cols]) * SCALE
        else:
            val = dot(GT[g % 2][...], PT[g % 2][:, cols])
        term[g, kind, pl.ds(k * 2, 4)] = val.astype(BF16).T.reshape(4, 128, 128)

    def grad_query(g, k):
        rows = pl.ds(k * ROWS, ROWS)
        val = dot(DS[g % 2][rows, :], kv[g, 0].reshape(2048, 128)) * SCALE
        for h in range(2):
            cols = pl.ds((g * 8 + 2 * k + h) * 128, 128)
            dq[:, cols] = val[h * 128 : h * 128 + 128].astype(BF16)

    def grad_step(g, k, j):
        if k < 2 and j % 2 == 0:
            grad_keys(g, (4, 0)[k] + j // 4 * 2, j // 2 % 2)
        if k >= 2 and j in (0, 4) and g != 2:
            grad_query(g, 2 * (k - 2) + j // 4)

    def unit(soft=None, ahead=None, grads=None, load=None):
        if ahead is not None:
            g, k = ahead
            cols = [pl.ds((g * 8 + 2 * k + h) * 128, 128) for h in range(2)]
            qb = jnp.concatenate([q[:, i] for i in cols], axis=0)
            gb = jnp.concatenate([gm[:, i] for i in cols], axis=0)
            qx = jnp.concatenate([qb, jnp.concatenate([bias[...]] * 2, axis=0)], axis=1)
            kt, vt = KT[g % 2], VT[g % 2]
            s_ref, dp_ref = S[k % 2], DP[k % 2]
        for j in range(8):
            if load is not None:
                for t in range(2 * j, 2 * j + 2):
                    load_block(load, t)
            if ahead is not None:
                cols = pl.ds(j * 256, 256)
                if j < 4:
                    s_ref[:, cols] = dot(qb, kt[0:128, cols])
                else:
                    s_ref[:, cols] = dot(qx, kt[:, cols])
                dp_ref[:, cols] = dot(gb, vt[:, cols])
            if soft is not None:
                for i in range(2 * j, 2 * j + 2):
                    soft_rows(soft[1] % 2, soft[0] % 2, soft[1], i)
            if grads is not None:
                grad_step(*grads, j)
            if soft is not None and j == 6:
                load_query(*soft)

    def back_copy(g, step):
        return pltpu.make_async_remote_copy(
            src_ref=term.at[g, :, 8 + step], dst_ref=back.at[g, step - 1],
            send_sem=d_send.at[g, step], recv_sem=d_recv.at[g, step],
            device_id=(c - step, r), device_id_type=MESH,
        )

    def send_back(g):
        for step in range(1, 8):
            @pl.when(step <= c)
            def _():
                back_copy(g, step).start()

    def finish_back(g):
        for step in range(1, 8):
            @pl.when(c + step < 8)
            def _():
                wait_bytes(back.at[g, step - 1], d_recv.at[g, step])
        cols = pl.ds(g * 128, 128)
        for kind, ref in ((0, drk_ref), (1, drv_ref)):
            total = term[g, kind, 8].astype(F32)
            for step in range(1, 8):
                total = total + back[g, step - 1, kind].astype(F32)
            ref[:, cols] = total.astype(BF16)

    def half_copy(g):
        return pltpu.make_async_remote_copy(
            src_ref=term.at[g, :, pl.ds(0, 8), other_half], dst_ref=half_in.at[g],
            send_sem=h_send.at[g], recv_sem=h_recv.at[g], device_id=sibling, device_id_type=MESH,
        )

    def z_copy(g, step):
        to_z = (z + step) % 4
        return pltpu.make_async_remote_copy(
            src_ref=half_sum.at[g, :, :, to_z], dst_ref=z_in.at[g, step - 1],
            send_sem=z_send.at[g, step], recv_sem=z_recv.at[g, step],
            device_id=(c, to_z * 4 + y_hi * 2 + core), device_id_type=MESH,
        )

    def add_halves(g):
        wait_bytes(half_in.at[g], h_recv.at[g])
        for kind in range(2):
            total = term[g, kind, pl.ds(0, 8), my_half, :].astype(F32) + half_in[g, kind].astype(F32)
            half_sum[g, kind] = total.astype(BF16).reshape(8, 4, 16, 128)
        for step in range(1, 4):
            z_copy(g, step).start()

    def add_z(g):
        for step in range(1, 4):
            wait_bytes(z_in.at[g, step - 1], z_recv.at[g, step])
        total = half_sum[g, :, :, z].astype(F32)
        for step in range(1, 4):
            total = total + z_in[g, step - 1].astype(F32)
        for cc in range(8):
            for yy in range(2):
                rows = slice(yy * 8, yy * 8 + 8)
                tile = jnp.concatenate([total[0, cc, rows], total[1, cc, rows]], axis=0)
                plane_out[cc, yy, g] = tile.astype(BF16)

    def plane_copy(step, heads, turn):
        to_c, to_y = plane_device(step)
        return pltpu.make_async_remote_copy(
            src_ref=plane_out.at[to_c, to_y, heads], dst_ref=plane_in.at[plane_id, heads],
            send_sem=x_send.at[turn], recv_sem=x_recv.at[turn],
            device_id=(to_c, z * 4 + to_y * 2 + core), device_id_type=MESH,
        )

    def plane_send(first, count, turn):
        heads = pl.ds(first, count)
        for step in range(1, 16):
            plane_copy(step, heads, turn).start()
        plane_in[plane_id, heads] = plane_out[c, y_hi, heads]

    def plane_finish(first, count, turn):
        for sem in (x_recv, x_send):
            wait_bytes(plane_in.at[pl.ds(0, 15), pl.ds(first, count)], sem.at[turn])
        for g in range(first, first + count):
            total = jnp.zeros((16, 128), F32)
            for i in range(16):
                total = total + plane_in[i, g].astype(F32)
            cols = pl.ds(g * 128, 128)
            dpk_ref[:, cols] = total[0:8].astype(BF16)
            dpv_ref[:, cols] = total[8:16].astype(BF16)

    def out_copy(g):
        cols = pl.ds(g * 1024, 1024)
        return pltpu.make_async_copy(dq.at[:, cols], dq_hbm.at[:, cols], out_sem.at[g])

    wait_bytes(prompt_bytes(0), p_recv.at[0])
    send_column(0)
    send_prompt(1)

    row = lax.broadcasted_iota(jnp.int32, (128, 1024), 0)
    key = lax.broadcasted_iota(jnp.int32, (128, 1024), 1)
    flag = ((key == row + 1) & (key < 128)) | ((row == 127) & (key >= (c + 1) * 128))
    flag = jnp.where(flag, 1.0, 0.0).astype(BF16)
    kt0[128:, 1024:] = flag
    kt1[128:, 1024:] = flag
    row = lax.broadcasted_iota(jnp.int32, (128, 128), 0)
    key = lax.broadcasted_iota(jnp.int32, (128, 128), 1)
    bias[...] = jnp.where(key >= row, -1e30, 0.0).astype(BF16)
    for step in range(1, 8):
        @pl.when(step > c)
        def _():
            for g in range(4):
                for kind in range(2):
                    kv[g, kind, 8 + step] = jnp.zeros((128, 128), BF16)

        @pl.when(c + step > 7)
        def _():
            for g in range(4):
                back[g, step - 1] = jnp.zeros((2, 128, 128), BF16)

    q_load.wait()
    g_load.wait()
    live = lax.broadcasted_iota(jnp.int32, (128, 128), 0) + c * 128 < len_ref[0]
    for t in range(32):
        cols = pl.ds(t * 128, 128)
        gm[:, cols] = jnp.where(live, gm[:, cols].astype(F32), 0.0).astype(BF16)

    relays(0, True)
    send_resp(1)
    send_resp(2)
    send_resp(3)
    forward_head(0)
    wait_bytes(prompt_bytes(1), p_recv.at[1])
    send_column(1)
    send_column(2)
    send_column(3)
    relays(1, True)
    await_head(0)
    for t in range(16):
        load_block(0, t)
    unit(ahead=(0, 0))
    for g in range(4):
        for k in range(4):
            if k == 1:
                if g < 3:
                    forward_head(g + 1)
                if g >= 1:
                    send_back(g - 1)
                if g >= 2:
                    add_z(g - 2)
            if (g, k) in RELAY_AT:
                relays(RELAY_AT[g, k], True)
            if k == 2 and g >= 1:
                half_copy(g - 1).start()
            if k == 3:
                if g < 3:
                    await_head(g + 1)
                if g >= 1:
                    add_halves(g - 1)
            last = k == 3
            ahead = (g, k + 1) if not last else (g + 1, 0) if g < 3 else None
            unit(
                soft=(g, k), ahead=ahead, grads=(g - 1, k) if g > 0 else None,
                load=g + 1 if last and g < 3 else None,
            )
        if g in (1, 2):
            out_copy(g - 1).start()

    for i in range(4):
        grad_keys(3, i // 2 * 2, i % 2)
    half_copy(3).start()
    for i in range(4):
        grad_keys(3, 4 + i // 2 * 2, i % 2)
    send_back(3)
    add_halves(3)
    add_z(2)
    plane_send(0, 3, 0)
    for k in range(4):
        grad_query(2, k)
    out_copy(2).start()
    for k in range(4):
        grad_query(3, k)
    out_copy(3).start()
    add_z(3)
    plane_send(3, 1, 1)
    for g in range(3):
        finish_back(g)
    plane_finish(0, 3, 0)
    finish_back(3)
    plane_finish(3, 1, 1)

    for turn in range(2):
        wait_bytes(prompt_bytes(turn), p_send.at[turn])
    for g in range(4):
        wait_bytes(column_bytes(g), a_send.at[g])
        wait_bytes(kv.at[g, :, pl.ds(0, 8), my_half], f_send.at[g])
        wait_bytes(half_in.at[g], h_send.at[g])
        for step in range(1, 4):
            @pl.when(x + step < 4)
            def _():
                wait_bytes(kv.at[g, :, 8], r_send.at[g, step])

        @pl.when(y_lo == 0)
        def _():
            wait_bytes(kv.at[g, :, 8], r_send.at[g, 4])

        relays(g, False)
        for step in range(1, 8):
            @pl.when(step <= c)
            def _():
                wait_bytes(term.at[g, :, 8 + step], d_send.at[g, step])
        for step in range(1, 4):
            wait_bytes(z_in.at[g, step - 1], z_send.at[g, step])
        out_copy(g).wait()


def hand_over(*refs):
    ins, outs, bufs, in_sem, out_sem = refs[:5], refs[5:10], refs[10:15], refs[15], refs[16]
    quarters = [(0, pl.ds(i * 1024, 1024)) for i in range(4)]
    parts = quarters + [(i, pl.ds(0, 512)) for i in range(1, 5)]
    reads = [
        pltpu.make_async_copy(ins[i].at[:, cols], bufs[i].at[:, cols], in_sem.at[n])
        for n, (i, cols) in enumerate(parts)
    ]
    writes = [
        pltpu.make_async_copy(bufs[i].at[:, cols], outs[i].at[:, cols], out_sem.at[n])
        for n, (i, cols) in enumerate(parts)
    ]
    for copy in reads:
        copy.start()
    for read, write in zip(reads, writes):
        read.wait()
        write.start()
    for copy in writes:
        copy.wait()


def per_device(query, prompt_keys, prompt_value_rows, response_keys, response_values, d_out, lengths):
    any_spec = pl.BlockSpec(memory_space=pl.ANY)
    vmem = pl.BlockSpec(memory_space=pltpu.VMEM)
    dma = pltpu.SemaphoreType.DMA
    scratch = [
        pltpu.VMEM((128, 4096), BF16),
        pltpu.VMEM((128, 4096), BF16),
        pltpu.VMEM((128, 4096), BF16),
        pltpu.VMEM((2, 128, 512), BF16),
        pltpu.VMEM((2, 128, 512), F32),
        pltpu.VMEM((4, 2, 16, 128, 128), BF16),
        pltpu.VMEM((4, 2, 16, 128, 128), BF16),
        pltpu.VMEM((4, 7, 2, 128, 128), BF16),
        pltpu.VMEM((4, 2, 8, 64, 128), BF16),
        pltpu.VMEM((4, 2, 8, 4, 16, 128), BF16),
        pltpu.VMEM((4, 3, 2, 8, 16, 128), BF16),
        pltpu.VMEM((8, 2, 4, 16, 128), BF16),
        pltpu.VMEM((16, 4, 16, 128), BF16),
    ]
    scratch += [pltpu.VMEM((1024, 2048), BF16)] * 4
    scratch += [pltpu.VMEM((ROWS, 2048), F32)] * 4
    scratch += [pltpu.VMEM((256, 2048), BF16)] * 2 + [pltpu.VMEM((128, 2048), BF16)] * 2
    scratch += [pltpu.VMEM((128, 1024), BF16)] * 4 + [pltpu.VMEM((128, 128), BF16)]
    scratch += [dma((12,)), dma((4,)), dma((2,)), dma((2,)), dma((4,)), dma((4,)), dma((4,)), dma((4,))]
    scratch += [dma((4, 8))] * 4 + [dma((4,))] * 2 + [dma((4, 4))] * 2 + [dma((2,))] * 2 + [dma((4, 5))]
    out = pl.pallas_call(
        kernel,
        out_shape=[
            jax.ShapeDtypeStruct((128, 4096), BF16),
            jax.ShapeDtypeStruct((128, 512), BF16),
            jax.ShapeDtypeStruct((128, 512), BF16),
            jax.ShapeDtypeStruct((8, 512), BF16),
            jax.ShapeDtypeStruct((8, 512), BF16),
        ],
        in_specs=[any_spec] * 6 + [pl.BlockSpec(memory_space=pltpu.SMEM)],
        out_specs=[any_spec] + [vmem] * 4,
        scratch_shapes=scratch,
        compiler_params=pltpu.CompilerParams(
            collective_id=0, has_side_effects=True, vmem_limit_bytes=62 * 2**20
        ),
    )(query[0], prompt_keys, prompt_value_rows, response_keys[0], response_values[0], d_out[0], lengths)
    d_query, d_rk, d_rv, d_pk, d_pv = pl.pallas_call(
        hand_over,
        out_shape=[jax.ShapeDtypeStruct(a.shape, a.dtype) for a in out],
        in_specs=[any_spec] * 5,
        out_specs=[any_spec] * 5,
        scratch_shapes=[pltpu.VMEM(a.shape, a.dtype) for a in out] + [dma((8,)), dma((8,))],
    )(*out)
    return d_query[None], d_rk[None], d_rv[None], d_pk, d_pv


def solution(mesh):
    return jax.shard_map(
        per_device,
        mesh=mesh,
        in_specs=(
            P("resp", "ctx", None),
            P("ctx", None),
            P("ctx", None),
            P("resp", "ctx", None),
            P("resp", "ctx", None),
            P("resp", "ctx", None),
            P("resp"),
        ),
        out_specs=(
            P("resp", "ctx", None),
            P("resp", "ctx", None),
            P("resp", "ctx", None),
            P(("ctx", "resp"), None),
            P(("ctx", "resp"), None),
        ),
        check_vma=False,
    )
```

```python
import functools

import jax
import jax.numpy as jnp
from jax import lax
from jax.experimental import pallas as pl
from jax.experimental.pallas import tpu as pltpu
from jax.sharding import PartitionSpec as P

F32, BF16 = jnp.float32, jnp.bfloat16
MESH = pl.DeviceIdType.MESH
SCALE = 128 ** -0.5
EXP2_SCALE = SCALE * 1.4426950408889634
BLOCK = 16
RELAY_AT = {(0, 2): 2, (1, 1): 3}
ROWS = 256


def dot(a, b):
    return lax.dot_general(a, b, (((1,), (0,)), ((), ())), preferred_element_type=F32)


def aligned(x, n):
    return x if isinstance(x, int) else pl.multiple_of(x, n)


def wait_bytes(ref, sem):
    pltpu.make_async_copy(ref, ref, sem).wait()


def kernel(
    q_hbm, pk_hbm, pv_hbm, rk_hbm, rv_hbm, g_hbm, len_ref,
    dq_hbm, drk_ref, drv_ref, dpk_ref, dpv_ref,
    q, gm, dq, pstage, pwide, kv, term, back, half_in, half_sum, z_in, plane_out, plane_in,
    pt0, pt1, ds0, ds1, s0, s1, dp0, dp1, kt0, kt1, vt0, vt1, qst0, qst1, gst0, gst1, bias,
    loc_sem, out_sem, p_send, p_recv, a_send, a_recv, f_send, f_recv, r_send, r_recv, d_send, d_recv,
    h_send, h_recv, z_send, z_recv, x_send, x_recv, y_send,
):
    c, r = lax.axis_index("ctx"), lax.axis_index("resp")
    y_lo, x = c // 4, c % 4
    z, y_hi, core = r // 4, (r // 2) % 2, r % 2
    sibling = (c, z * 4 + y_hi * 2 + 1 - core)
    other = 1 - core
    PT, DS, KT, VT, S, DP = [pt0, pt1], [ds0, ds1], [kt0, kt1], [vt0, vt1], [s0, s1], [dp0, dp1]
    QT, GT = [qst0, qst1], [gst0, gst1]

    loads = []
    for g in range(4):
        cols = pl.ds(g * 128, 128)
        loads.append(pltpu.make_async_copy(rk_hbm.at[:, cols], kv.at[g, 0, 8], loc_sem.at[len(loads)]))
        loads.append(pltpu.make_async_copy(rv_hbm.at[:, cols], kv.at[g, 1, 8], loc_sem.at[len(loads)]))
    loads.append(pltpu.make_async_copy(pk_hbm, pstage.at[0], loc_sem.at[8]))
    loads.append(pltpu.make_async_copy(pv_hbm, pstage.at[1], loc_sem.at[9]))
    q_load = pltpu.make_async_copy(q_hbm, q, loc_sem.at[10])
    g_load = pltpu.make_async_copy(g_hbm, gm, loc_sem.at[11])
    for copy in loads[8:] + loads[:8]:
        copy.start()
    q_load.start()
    g_load.start()

    barrier = pltpu.get_barrier_semaphore()
    plane_id = c * 2 + y_hi

    def plane_device(step):
        to = (plane_id + step) % 16
        return to // 2, to % 2

    for step in range(1, 16):
        to_c, to_y = plane_device(step)
        pl.semaphore_signal(barrier, inc=1, device_id=(to_c, z * 4 + to_y * 2 + core), device_id_type=MESH)
    for step in range(1, 4):
        to_z = (z + step) % 4
        pl.semaphore_signal(barrier, inc=1, device_id=(c, to_z * 4 + y_hi * 2 + core), device_id_type=MESH)
    pl.semaphore_signal(barrier, inc=1, device_id=sibling, device_id_type=MESH)

    my_half = pl.ds(pl.multiple_of(core * 64, 64), 64)
    other_half = pl.ds(pl.multiple_of(other * 64, 64), 64)
    my_rows = pl.ds(pl.multiple_of(core * 64 + z * 16, 16), 16)
    far_z = (z + 2) % 4
    far_rows = pl.ds(pl.multiple_of(core * 64 + far_z * 16, 16), 16)
    loads[8].wait()
    loads[9].wait()
    for kind in range(2):
        pwide[kind] = pstage[kind].astype(F32)
        for zz, rows in ((z, my_rows), (far_z, far_rows)):
            parts = [pwide[kind, pl.ds(pl.multiple_of((zz * 4 + yy * 2 + core) * 8, 8), 8), :] for yy in range(2)]
            mine = jnp.concatenate(parts, axis=0).astype(BF16)
            for g in range(4):
                kv[g, kind, c, rows, :] = mine[:, g * 128 : g * 128 + 128]
    pl.semaphore_wait(barrier, 19)

    def prompt_copy(turn, step, rows):
        heads = pl.ds(0, 1) if turn == 0 else pl.ds(1, 3)
        to_c = (c + step) % 8
        to_y = jnp.where(to_c // 4 == y_lo, y_hi, 1 - y_hi)
        return pltpu.make_async_remote_copy(
            src_ref=kv.at[heads, :, c, rows], dst_ref=kv.at[heads, :, c, rows],
            send_sem=p_send.at[turn], recv_sem=p_recv.at[turn],
            device_id=(to_c, z * 4 + to_y * 2 + core), device_id_type=MESH,
        )

    def prompt_bytes(turn):
        heads = pl.ds(0, 1) if turn == 0 else pl.ds(1, 3)
        return kv.at[heads, :, pl.ds(0, 7), pl.ds(0, 32)]

    def column_copy(g, step):
        to_z = (z + step) % 4
        return pltpu.make_async_remote_copy(
            src_ref=kv.at[g, :, pl.ds(0, 8), my_rows], dst_ref=kv.at[g, :, pl.ds(0, 8), my_rows],
            send_sem=a_send.at[g], recv_sem=a_recv.at[g],
            device_id=(c, to_z * 4 + y_hi * 2 + core), device_id_type=MESH,
        )

    def column_bytes(g):
        return kv.at[g, :, pl.ds(0, 8), pl.ds(0, 32)]

    def forward_copy(g):
        return pltpu.make_async_remote_copy(
            src_ref=kv.at[g, :, pl.ds(0, 8), my_half], dst_ref=kv.at[g, :, pl.ds(0, 8), my_half],
            send_sem=f_send.at[g], recv_sem=f_recv.at[g], device_id=sibling, device_id_type=MESH,
        )

    def resp_copy(g, step):
        return pltpu.make_async_remote_copy(
            src_ref=kv.at[g, :, 8], dst_ref=kv.at[g, :, 8 + step],
            send_sem=r_send.at[g, step], recv_sem=r_recv.at[g, step],
            device_id=(c + step, r), device_id_type=MESH,
        )

    def send_prompt(turn):
        for step in range(1, 8):
            prompt_copy(turn, step, my_rows).start()
            prompt_copy(turn, step, far_rows).start()

    def send_column(g):
        for step in (1, 3):
            column_copy(g, step).start()

    def forward_head(g):
        wait_bytes(column_bytes(g), a_recv.at[g])
        forward_copy(g).start()

    def send_resp(g):
        for step in range(1, 4):
            @pl.when(x + step < 4)
            def _():
                resp_copy(g, step).start()

        @pl.when(y_lo == 0)
        def _():
            resp_copy(g, 4).start()

    def down_copy(g, step):
        return pltpu.make_async_remote_copy(
            src_ref=kv.at[g, :, 8 + step], dst_ref=kv.at[g, :, 12 + step],
            send_sem=y_send.at[g, step], recv_sem=r_recv.at[g, 4 + step],
            device_id=(c + 4, r), device_id_type=MESH,
        )

    def side_copy(g, step):
        return pltpu.make_async_remote_copy(
            src_ref=kv.at[g, :, 12], dst_ref=kv.at[g, :, 12 - step],
            send_sem=y_send.at[g, step], recv_sem=r_recv.at[g, 4 - step],
            device_id=(c - step, r), device_id_type=MESH,
        )

    def wrap_copy(g):
        return pltpu.make_async_remote_copy(
            src_ref=kv.at[g, :, 12], dst_ref=kv.at[g, :, 15],
            send_sem=y_send.at[g, 4], recv_sem=r_recv.at[g, 7],
            device_id=(c + 3, r), device_id_type=MESH,
        )

    def relays(g, act):
        for step in range(1, 4):
            @pl.when((y_lo == 0) & (step <= x))
            def _():
                if act:
                    wait_bytes(kv.at[g, :, 8 + step], r_recv.at[g, step])

            if step < 3:
                @pl.when((y_lo == 0) & (step <= x))
                def _():
                    if act:
                        down_copy(g, step).start()
                    else:
                        wait_bytes(kv.at[g, :, 8], y_send.at[g, step])

        @pl.when(y_lo == 1)
        def _():
            if act:
                wait_bytes(kv.at[g, :, 12], r_recv.at[g, 4])

        for step in range(1, 4):
            @pl.when((y_lo == 1) & (step <= x))
            def _():
                if act:
                    side_copy(g, step).start()
                else:
                    wait_bytes(kv.at[g, :, 8], y_send.at[g, step])

        @pl.when((y_lo == 1) & (x == 0))
        def _():
            if act:
                wrap_copy(g).start()
            else:
                wait_bytes(kv.at[g, :, 8], y_send.at[g, 4])

    def await_head(g):
        for step in (1, 2, 3, 5, 6, 7):
            @pl.when((y_lo == 1) & (step <= c))
            def _():
                wait_bytes(kv.at[g, :, 8 + step], r_recv.at[g, step])
        wait_bytes(kv.at[g, :, pl.ds(0, 8), other_half], f_recv.at[g])

    send_prompt(0)
    for copy in loads[:8]:
        copy.wait()
    send_resp(0)

    def load_block(g, t):
        rows = pl.ds(t * 128, 128)
        KT[g % 2][0:128, rows] = kv[g, 0, t].T
        VT[g % 2][:, rows] = kv[g, 1, t].T

    def load_query(g, k):
        for h in range(2 * k, 2 * k + 2):
            cols = pl.ds((g * 8 + h) * 128, 128)
            QT[g % 2][:, pl.ds(h * 128, 128)] = q[:, cols].T
            GT[g % 2][:, pl.ds(h * 128, 128)] = gm[:, cols].T

    def soft_rows(buf, b, k, j):
        rows = pl.ds(j * BLOCK, BLOCK)
        s = S[buf][rows, :]
        m = jnp.max(s, axis=1, keepdims=True)
        dp = DP[buf][rows, :]
        e = jnp.exp2((s - m) * EXP2_SCALE)
        inv = 1.0 / jnp.sum(e, axis=1, keepdims=True)
        delta = jnp.sum(e * dp, axis=1, keepdims=True) * inv
        p = e * inv
        out = pl.ds(k * ROWS + j * BLOCK, BLOCK)
        PT[b][out, :] = p.astype(BF16)
        DS[b][out, :] = (p * (dp - delta)).astype(BF16)

    def grad_keys(g, k, kind):
        cols = pl.ds(k * 256, 512)
        if kind == 0:
            val = dot(QT[g % 2][...], DS[g % 2][:, cols]) * SCALE
        else:
            val = dot(GT[g % 2][...], PT[g % 2][:, cols])
        term[g, kind, pl.ds(k * 2, 4)] = val.astype(BF16).T.reshape(4, 128, 128)

    def grad_query(g, k):
        rows = pl.ds(k * ROWS, ROWS)
        val = dot(DS[g % 2][rows, :], kv[g, 0].reshape(2048, 128)) * SCALE
        for h in range(2):
            cols = pl.ds((g * 8 + 2 * k + h) * 128, 128)
            dq[:, cols] = val[h * 128 : h * 128 + 128].astype(BF16)

    def grad_step(g, k, j):
        if k < 2 and j % 2 == 0:
            grad_keys(g, (4, 0)[k] + j // 4 * 2, j // 2 % 2)
        if k >= 2 and j in (0, 4) and g != 2:
            grad_query(g, 2 * (k - 2) + j // 4)

    def unit(soft=None, ahead=None, grads=None, load=None):
        if ahead is not None:
            g, k = ahead
            cols = [pl.ds((g * 8 + 2 * k + h) * 128, 128) for h in range(2)]
            qb = jnp.concatenate([q[:, i] for i in cols], axis=0)
            gb = jnp.concatenate([gm[:, i] for i in cols], axis=0)
            qx = jnp.concatenate([qb, jnp.concatenate([bias[...]] * 2, axis=0)], axis=1)
            kt, vt = KT[g % 2], VT[g % 2]
            s_ref, dp_ref = S[k % 2], DP[k % 2]
        for j in range(8):
            if load is not None:
                for t in range(2 * j, 2 * j + 2):
                    load_block(load, t)
            if ahead is not None:
                cols = pl.ds(j * 256, 256)
                if j < 4:
                    s_ref[:, cols] = dot(qb, kt[0:128, cols])
                else:
                    s_ref[:, cols] = dot(qx, kt[:, cols])
                dp_ref[:, cols] = dot(gb, vt[:, cols])
            if soft is not None:
                for i in range(2 * j, 2 * j + 2):
                    soft_rows(soft[1] % 2, soft[0] % 2, soft[1], i)
            if grads is not None:
                grad_step(*grads, j)
            if soft is not None and j == 6:
                load_query(*soft)

    def back_copy(g, step):
        return pltpu.make_async_remote_copy(
            src_ref=term.at[g, :, 8 + step], dst_ref=back.at[g, step - 1],
            send_sem=d_send.at[g, step], recv_sem=d_recv.at[g, step],
            device_id=(c - step, r), device_id_type=MESH,
        )

    def send_back(g):
        for step in range(1, 8):
            @pl.when(step <= c)
            def _():
                back_copy(g, step).start()

    def finish_back(g):
        for step in range(1, 8):
            @pl.when(c + step < 8)
            def _():
                wait_bytes(back.at[g, step - 1], d_recv.at[g, step])
        cols = pl.ds(g * 128, 128)
        for kind, ref in ((0, drk_ref), (1, drv_ref)):
            total = term[g, kind, 8].astype(F32)
            for step in range(1, 8):
                total = total + back[g, step - 1, kind].astype(F32)
            ref[:, cols] = total.astype(BF16)

    def half_copy(g):
        return pltpu.make_async_remote_copy(
            src_ref=term.at[g, :, pl.ds(0, 8), other_half], dst_ref=half_in.at[g],
            send_sem=h_send.at[g], recv_sem=h_recv.at[g], device_id=sibling, device_id_type=MESH,
        )

    def z_copy(g, step):
        to_z = (z + step) % 4
        return pltpu.make_async_remote_copy(
            src_ref=half_sum.at[g, :, :, to_z], dst_ref=z_in.at[g, step - 1],
            send_sem=z_send.at[g, step], recv_sem=z_recv.at[g, step],
            device_id=(c, to_z * 4 + y_hi * 2 + core), device_id_type=MESH,
        )

    def add_halves(g):
        wait_bytes(half_in.at[g], h_recv.at[g])
        for kind in range(2):
            total = term[g, kind, pl.ds(0, 8), my_half, :].astype(F32) + half_in[g, kind].astype(F32)
            half_sum[g, kind] = total.astype(BF16).reshape(8, 4, 16, 128)
        for step in range(1, 4):
            z_copy(g, step).start()

    def add_z(g):
        for step in range(1, 4):
            wait_bytes(z_in.at[g, step - 1], z_recv.at[g, step])
        total = half_sum[g, :, :, z].astype(F32)
        for step in range(1, 4):
            total = total + z_in[g, step - 1].astype(F32)
        for cc in range(8):
            for yy in range(2):
                rows = slice(yy * 8, yy * 8 + 8)
                tile = jnp.concatenate([total[0, cc, rows], total[1, cc, rows]], axis=0)
                plane_out[cc, yy, g] = tile.astype(BF16)

    def plane_copy(step, heads, turn):
        to_c, to_y = plane_device(step)
        return pltpu.make_async_remote_copy(
            src_ref=plane_out.at[to_c, to_y, heads], dst_ref=plane_in.at[plane_id, heads],
            send_sem=x_send.at[turn], recv_sem=x_recv.at[turn],
            device_id=(to_c, z * 4 + to_y * 2 + core), device_id_type=MESH,
        )

    def plane_send(first, count, turn):
        heads = pl.ds(first, count)
        for step in range(1, 16):
            plane_copy(step, heads, turn).start()
        plane_in[plane_id, heads] = plane_out[c, y_hi, heads]

    def plane_finish(first, count, turn):
        for sem in (x_recv, x_send):
            wait_bytes(plane_in.at[pl.ds(0, 15), pl.ds(first, count)], sem.at[turn])
        for g in range(first, first + count):
            total = jnp.zeros((16, 128), F32)
            for i in range(16):
                total = total + plane_in[i, g].astype(F32)
            cols = pl.ds(g * 128, 128)
            dpk_ref[:, cols] = total[0:8].astype(BF16)
            dpv_ref[:, cols] = total[8:16].astype(BF16)

    def out_copy(g):
        cols = pl.ds(g * 1024, 1024)
        return pltpu.make_async_copy(dq.at[:, cols], dq_hbm.at[:, cols], out_sem.at[g])

    wait_bytes(prompt_bytes(0), p_recv.at[0])
    send_column(0)
    send_prompt(1)

    relays(0, True)
    row = lax.broadcasted_iota(jnp.int32, (128, 1024), 0)
    key = lax.broadcasted_iota(jnp.int32, (128, 1024), 1)
    flag = ((key == row + 1) & (key < 128)) | ((row == 127) & (key >= (c + 1) * 128))
    flag = jnp.where(flag, 1.0, 0.0).astype(BF16)
    kt0[128:, 1024:] = flag
    kt1[128:, 1024:] = flag
    row = lax.broadcasted_iota(jnp.int32, (128, 128), 0)
    key = lax.broadcasted_iota(jnp.int32, (128, 128), 1)
    bias[...] = jnp.where(key >= row, -1e30, 0.0).astype(BF16)
    for step in range(1, 8):
        @pl.when(step > c)
        def _():
            for g in range(4):
                for kind in range(2):
                    kv[g, kind, 8 + step] = jnp.zeros((128, 128), BF16)

        @pl.when(c + step > 7)
        def _():
            for g in range(4):
                back[g, step - 1] = jnp.zeros((2, 128, 128), BF16)

    q_load.wait()
    g_load.wait()
    live = lax.broadcasted_iota(jnp.int32, (128, 128), 0) + c * 128 < len_ref[0]
    for t in range(32):
        cols = pl.ds(t * 128, 128)
        gm[:, cols] = jnp.where(live, gm[:, cols].astype(F32), 0.0).astype(BF16)

    send_resp(1)
    send_resp(2)
    send_resp(3)
    forward_head(0)
    wait_bytes(prompt_bytes(1), p_recv.at[1])
    send_column(1)
    send_column(2)
    send_column(3)
    relays(1, True)
    await_head(0)
    for t in range(16):
        load_block(0, t)
    unit(ahead=(0, 0))
    for g in range(4):
        for k in range(4):
            if k == 1:
                if g < 3:
                    forward_head(g + 1)
                if g >= 1:
                    send_back(g - 1)
                if g >= 2:
                    add_z(g - 2)
            if (g, k) in RELAY_AT:
                relays(RELAY_AT[g, k], True)
            if k == 2 and g >= 1:
                half_copy(g - 1).start()
            if k == 3:
                if g < 3:
                    await_head(g + 1)
                if g >= 1:
                    add_halves(g - 1)
            last = k == 3
            ahead = (g, k + 1) if not last else (g + 1, 0) if g < 3 else None
            unit(
                soft=(g, k), ahead=ahead, grads=(g - 1, k) if g > 0 else None,
                load=g + 1 if last and g < 3 else None,
            )
        if g in (1, 2):
            out_copy(g - 1).start()

    for i in range(4):
        grad_keys(3, i // 2 * 2, i % 2)
    half_copy(3).start()
    for i in range(4):
        grad_keys(3, 4 + i // 2 * 2, i % 2)
    send_back(3)
    add_halves(3)
    add_z(2)
    plane_send(0, 3, 0)
    for k in range(4):
        grad_query(2, k)
    out_copy(2).start()
    for k in range(4):
        grad_query(3, k)
    out_copy(3).start()
    add_z(3)
    plane_send(3, 1, 1)
    for g in range(3):
        finish_back(g)
    plane_finish(0, 3, 0)
    finish_back(3)
    plane_finish(3, 1, 1)

    for turn in range(2):
        wait_bytes(prompt_bytes(turn), p_send.at[turn])
    for g in range(4):
        wait_bytes(column_bytes(g), a_send.at[g])
        wait_bytes(kv.at[g, :, pl.ds(0, 8), my_half], f_send.at[g])
        wait_bytes(half_in.at[g], h_send.at[g])
        for step in range(1, 4):
            @pl.when(x + step < 4)
            def _():
                wait_bytes(kv.at[g, :, 8], r_send.at[g, step])

        @pl.when(y_lo == 0)
        def _():
            wait_bytes(kv.at[g, :, 8], r_send.at[g, 4])

        relays(g, False)
        for step in range(1, 8):
            @pl.when(step <= c)
            def _():
                wait_bytes(term.at[g, :, 8 + step], d_send.at[g, step])
        for step in range(1, 4):
            wait_bytes(z_in.at[g, step - 1], z_send.at[g, step])
        out_copy(g).wait()


def hand_over(*refs):
    ins, outs, bufs, in_sem, out_sem = refs[:5], refs[5:10], refs[10:15], refs[15], refs[16]
    quarters = [(0, pl.ds(i * 1024, 1024)) for i in range(4)]
    parts = quarters + [(i, pl.ds(0, 512)) for i in range(1, 5)]
    reads = [
        pltpu.make_async_copy(ins[i].at[:, cols], bufs[i].at[:, cols], in_sem.at[n])
        for n, (i, cols) in enumerate(parts)
    ]
    writes = [
        pltpu.make_async_copy(bufs[i].at[:, cols], outs[i].at[:, cols], out_sem.at[n])
        for n, (i, cols) in enumerate(parts)
    ]
    for copy in reads:
        copy.start()
    for read, write in zip(reads, writes):
        read.wait()
        write.start()
    for copy in writes:
        copy.wait()


def per_device(query, prompt_keys, prompt_value_rows, response_keys, response_values, d_out, lengths):
    any_spec = pl.BlockSpec(memory_space=pl.ANY)
    vmem = pl.BlockSpec(memory_space=pltpu.VMEM)
    dma = pltpu.SemaphoreType.DMA
    scratch = [
        pltpu.VMEM((128, 4096), BF16),
        pltpu.VMEM((128, 4096), BF16),
        pltpu.VMEM((128, 4096), BF16),
        pltpu.VMEM((2, 128, 512), BF16),
        pltpu.VMEM((2, 128, 512), F32),
        pltpu.VMEM((4, 2, 16, 128, 128), BF16),
        pltpu.VMEM((4, 2, 16, 128, 128), BF16),
        pltpu.VMEM((4, 7, 2, 128, 128), BF16),
        pltpu.VMEM((4, 2, 8, 64, 128), BF16),
        pltpu.VMEM((4, 2, 8, 4, 16, 128), BF16),
        pltpu.VMEM((4, 3, 2, 8, 16, 128), BF16),
        pltpu.VMEM((8, 2, 4, 16, 128), BF16),
        pltpu.VMEM((16, 4, 16, 128), BF16),
    ]
    scratch += [pltpu.VMEM((1024, 2048), BF16)] * 4
    scratch += [pltpu.VMEM((ROWS, 2048), F32)] * 4
    scratch += [pltpu.VMEM((256, 2048), BF16)] * 2 + [pltpu.VMEM((128, 2048), BF16)] * 2
    scratch += [pltpu.VMEM((128, 1024), BF16)] * 4 + [pltpu.VMEM((128, 128), BF16)]
    scratch += [dma((12,)), dma((4,)), dma((2,)), dma((2,)), dma((4,)), dma((4,)), dma((4,)), dma((4,))]
    scratch += [dma((4, 8))] * 4 + [dma((4,))] * 2 + [dma((4, 4))] * 2 + [dma((2,))] * 2 + [dma((4, 5))]
    out = pl.pallas_call(
        kernel,
        out_shape=[
            jax.ShapeDtypeStruct((128, 4096), BF16),
            jax.ShapeDtypeStruct((128, 512), BF16),
            jax.ShapeDtypeStruct((128, 512), BF16),
            jax.ShapeDtypeStruct((8, 512), BF16),
            jax.ShapeDtypeStruct((8, 512), BF16),
        ],
        in_specs=[any_spec] * 6 + [pl.BlockSpec(memory_space=pltpu.SMEM)],
        out_specs=[any_spec] + [vmem] * 4,
        scratch_shapes=scratch,
        compiler_params=pltpu.CompilerParams(
            collective_id=0, has_side_effects=True, vmem_limit_bytes=62 * 2**20
        ),
    )(query[0], prompt_keys, prompt_value_rows, response_keys[0], response_values[0], d_out[0], lengths)
    d_query, d_rk, d_rv, d_pk, d_pv = pl.pallas_call(
        hand_over,
        out_shape=[jax.ShapeDtypeStruct(a.shape, a.dtype) for a in out],
        in_specs=[any_spec] * 5,
        out_specs=[any_spec] * 5,
        scratch_shapes=[pltpu.VMEM(a.shape, a.dtype) for a in out] + [dma((8,)), dma((8,))],
    )(*out)
    return d_query[None], d_rk[None], d_rv[None], d_pk, d_pv


def solution(mesh):
    return jax.shard_map(
        per_device,
        mesh=mesh,
        in_specs=(
            P("resp", "ctx", None),
            P("ctx", None),
            P("ctx", None),
            P("resp", "ctx", None),
            P("resp", "ctx", None),
            P("resp", "ctx", None),
            P("resp"),
        ),
        out_specs=(
            P("resp", "ctx", None),
            P("resp", "ctx", None),
            P("resp", "ctx", None),
            P(("ctx", "resp"), None),
            P(("ctx", "resp"), None),
        ),
        check_vma=False,
    )
```
